32 devices in a mesh: groups: 2 (over y), space: 4 (over x, core), dp: 4 (over z).
Axes of the slice: x: 2, y: 2, z: 4, core: 2. Of those that a mesh axis runs over, the one named last changes fastest.
Arguments:
- inputs: bfloat16 [8, 8, 128, 768], P(('groups', 'dp'), 'space'), parts along dimension 0, may hold values from -6 to 6
- cotangent: bfloat16 [8, 8, 128, 768], P(('groups', 'dp'), 'space'), parts along dimension 0, may hold values from -6 to 6
- kernel_raw: float32 [768, 1152], P('dp'), may hold values from -0.1875 to 0.1875
- kernel_gain: float32 [768], P('dp'), may hold values from 0.25 to 1.75
Outputs:
- grad_inputs: bfloat16 [8, 8, 128, 768], P(('groups', 'dp'), 'space'), parts along dimension 0
- grad_raw: float32 [1536, 1152], P(('groups', 'dp')), parts along dimension 0
- grad_gain: float32 [1536], P(('groups', 'dp')), parts along dimension 0
The draws below stay inside these ranges and needn't reach their ends.
There are 2 independent parts, one for each index of `groups`. The reference program is written for one: setup_inputs(seed, part) draws one part's arguments, and reference() takes and returns one part's arrays. A program takes and returns all parts, laid end to end along the dimension named above; an argument that names none is the same for every part. Nothing has to cross between parts.
All inputs are finite; a program needn't handle non-finite values.
Results may differ from the reference program's by a relative error of at most 0.0052.
Values may be sent and summed in bfloat16 or wider, within the bound.
A program may use at most 64 MiB of HBM per device.

```python
import math
import jax
import jax.numpy as jnp
from jax import lax

CH = 768
GW = 128
FAN = 1152
COLS = 128
IMAGES = 4
ROWS = 8


def levels(rng, shape, pieces, least, top_value):
    factor_of, own = 1.0, jax.random.fold_in(rng, 6)
    for dim, blocks in pieces:
        heights = jnp.exp(jax.random.uniform(jax.random.fold_in(own, dim), (blocks,), jnp.float32, least / len(pieces), top_value / len(pieces)))
        factor_of = factor_of * jnp.repeat(heights, shape[dim] // blocks).reshape([-1 if axis == dim else 1 for axis in range(len(shape))])
    return factor_of


def bell_draw(key, extent, width, limit, cuts=(), dtype=jnp.bfloat16):
    drawn = jax.random.normal(key, extent, jnp.float32) * width
    if len(cuts) > 0:
        drawn = levels(key, extent, cuts, -0.22, 0.18) * drawn
    return jnp.clip(drawn, min=-limit, max=limit).astype(dtype)


def setup_inputs(seed: int = 0, part: int = 0) -> dict:
    arg_keys = jax.random.split(jax.random.key(seed), 5)
    part_keys = jax.random.split(jax.random.fold_in(arg_keys[4], part), 5)
    inputs = bell_draw(part_keys[0], (IMAGES, ROWS, COLS, CH), 1.0, 6.0, ((0, 4), (1, 4)))
    cotangent = bell_draw(part_keys[1], (IMAGES, ROWS, COLS, CH), 1.0, 6.0, ((0, 4), (1, 4)))
    kernel_raw = bell_draw(arg_keys[2], (CH, FAN), FAN ** -0.5, 0.1875, ((0, 4),), jnp.float32)
    kernel_gain = jnp.clip(1.0 + 0.15 * jax.random.normal(arg_keys[3], (CH,), jnp.float32), 0.25, 1.75)
    return dict(inputs=inputs, cotangent=cotangent, kernel_raw=kernel_raw, kernel_gain=kernel_gain)


act_gain = 1.7015
alpha_skip = 0.2

def standardize(kernel_raw, kernel_gain):
    row_mean = lax.optimization_barrier(jnp.mean(kernel_raw, axis=1, keepdims=True))
    centred = kernel_raw - row_mean
    row_var = lax.optimization_barrier(jnp.mean(centred * centred, axis=1, keepdims=True))
    unit = centred * lax.rsqrt(row_var + 1e-05)
    return kernel_gain[:, None] * unit / math.sqrt(FAN)

def activate(value_in):
    return act_gain * jax.nn.gelu(value_in, approximate=False)

def convolve(hidden_in, kernel_hwio):
    return lax.conv_general_dilated(hidden_in, kernel_hwio, (1, 1), ((1, 1), (1, 1)), dimension_numbers=('NHWC', 'HWIO', 'NHWC'), feature_group_count=CH // GW, precision=lax.Precision.HIGHEST)

def reference(inputs, cotangent, kernel_raw, kernel_gain):
    inputs_wide = inputs.astype(jnp.float32)
    hidden = activate(inputs_wide).astype(jnp.bfloat16)
    standard = standardize(kernel_raw, kernel_gain).astype(jnp.bfloat16)
    grad_conv = (alpha_skip * cotangent.astype(jnp.float32)).astype(jnp.bfloat16)
    kernel_hwio = standard.astype(jnp.float32).reshape(CH, 3, 3, GW).transpose(1, 2, 3, 0)
    unused_out, pull_conv = jax.vjp(convolve, hidden.astype(jnp.float32), kernel_hwio)
    grad_hidden, grad_kernel = pull_conv(grad_conv.astype(jnp.float32))
    grad_standard = grad_kernel.transpose(3, 0, 1, 2).reshape(CH, FAN) / IMAGES
    unused_std, pull_ws = jax.vjp(standardize, kernel_raw, kernel_gain)
    grad_raw, grad_gain = pull_ws(grad_standard)
    unused_act, pull_act = jax.vjp(activate, inputs_wide)
    grad_inputs = cotangent.astype(jnp.float32) + pull_act(grad_hidden)[0]
    return (grad_inputs.astype(jnp.bfloat16), grad_raw, grad_gain)
```

```python
import functools
import math

import jax
import jax.numpy as jnp
from jax import lax
from jax.experimental import pallas as pl
from jax.experimental.pallas import tpu as pltpu
from jax.sharding import PartitionSpec as P

act_gain = 1.7015
alpha_skip = 0.2


def padded_2(value, sides, width):
    for axis, dim in sides:
        size, length = (lax.axis_size(axis), value.shape[dim])
        up = [(i, (i + 1) % size) for i in range(size - 1)]
        down = [(j, i) for i, j in up]
        last = lax.slice_in_dim(value, length - width, length, axis=dim)
        first = lax.slice_in_dim(value, 0, width, axis=dim)
        before = lax.ppermute(last, axis, up)
        after = lax.ppermute(first, axis, down)
        value = jnp.concatenate([before, value, after], axis=dim)
    return value


def activate(value_in):
    return act_gain * jax.nn.gelu(value_in, approximate=False)


def ws_parts(kernel_rows):
    row_mean = jnp.mean(kernel_rows, axis=1, keepdims=True)
    centred = kernel_rows - row_mean
    row_var = jnp.mean(centred * centred, axis=1, keepdims=True)
    inv_std = lax.rsqrt(row_var + 1e-05)
    return (centred * inv_std, inv_std)


def ws_back(grad_standard, unit, inv_std, gains):
    fan_scale = 1.0 / math.sqrt(unit.shape[1])
    grad_gain = jnp.sum(grad_standard * unit, axis=1) * fan_scale
    grad_unit = grad_standard * gains[:, None] * fan_scale
    centre_term = jnp.mean(grad_unit, axis=1, keepdims=True)
    along_term = jnp.mean(grad_unit * unit, axis=1, keepdims=True)
    grad_raw = inv_std * (grad_unit - centre_term - unit * along_term)
    return (grad_raw, grad_gain)


def local(inputs, cotangent, kernel_raw, kernel_gain):
    images, band_rows, band_cols, chan_count = inputs.shape
    fan_size = kernel_raw.shape[1]
    group_width = fan_size // 9
    group_count = chan_count // group_width
    fan_scale = 1.0 / math.sqrt(fan_size)
    inputs_wide = inputs.astype(jnp.float32)
    hidden = activate(inputs_wide).astype(jnp.bfloat16)
    grad_conv = (alpha_skip * cotangent.astype(jnp.float32)).astype(jnp.bfloat16)
    stacked = jnp.stack([hidden, grad_conv])
    rimmed = padded_2(stacked, (("space", 2),), 1)
    padded = jnp.pad(rimmed, ((0, 0), (0, 0), (0, 0), (1, 1), (0, 0)))
    hidden_pad = padded[0]
    grad_pad = padded[1]
    unit, inv_std = ws_parts(kernel_raw)
    standard_rows = (kernel_gain[:, None] * unit * fan_scale).astype(jnp.bfloat16)
    standard = lax.all_gather(standard_rows, "dp", axis=0, tiled=True)
    tap_kernels = standard.reshape(group_count, group_width, 3, 3, group_width)
    count = images * band_rows * band_cols
    grad_flat = grad_conv.reshape(count, group_count, group_width)
    grad_hidden = jnp.zeros((count, group_count, group_width), jnp.float32)
    tap_grads = []
    for tap_row in range(3):
        backed_cols = []
        for tap_col in range(3):
            shifted = hidden_pad[:, tap_row : tap_row + band_rows, tap_col : tap_col + band_cols]
            shifted = shifted.reshape(count, group_count, group_width)
            tap_grads.append(
                jnp.einsum("mgo,mgi->goi", grad_flat, shifted, preferred_element_type=jnp.float32)
            )
            backed = grad_pad[
                :, 2 - tap_row : 2 - tap_row + band_rows, 2 - tap_col : 2 - tap_col + band_cols
            ]
            backed_cols.append(backed.reshape(count, group_count, group_width))
        backed_row = jnp.stack(backed_cols, axis=2)
        grad_hidden = grad_hidden + jnp.einsum(
            "mgbo,gobi->mgi",
            backed_row,
            tap_kernels[:, :, tap_row],
            preferred_element_type=jnp.float32,
        )
    total_images = images * lax.axis_size("dp")
    grad_standard = jnp.stack(tap_grads, axis=2).reshape(chan_count, fan_size) * (
        1.0 / total_images
    )
    unused_act, pull_act = jax.vjp(activate, inputs_wide)
    grad_inputs = cotangent.astype(jnp.float32) + pull_act(grad_hidden.reshape(inputs.shape))[0]
    band_count = lax.axis_size("space")
    data_count = lax.axis_size("dp")
    owner_rows = kernel_raw.shape[0]
    piece_rows = owner_rows // band_count
    ordered = grad_standard.reshape(data_count, band_count, piece_rows, fan_size)
    ordered = ordered.transpose(1, 0, 2, 3).reshape(chan_count, fan_size)
    piece = lax.psum_scatter(ordered, ("space", "dp"), scatter_dimension=0, tiled=True)
    start = lax.axis_index("space") * piece_rows
    unit_piece = lax.dynamic_slice_in_dim(unit, start, piece_rows, 0)
    inv_piece = lax.dynamic_slice_in_dim(inv_std, start, piece_rows, 0)
    gain_piece = lax.dynamic_slice_in_dim(kernel_gain, start, piece_rows, 0)
    raw_piece, gain_grad_piece = ws_back(piece, unit_piece, inv_piece, gain_piece)
    grad_raw, grad_gain = (
        lax.all_gather(raw_piece, "space", axis=0, tiled=True),
        lax.all_gather(gain_grad_piece, "space", axis=0, tiled=True),
    )
    return (grad_inputs.astype(jnp.bfloat16), grad_raw, grad_gain)


MESH = pl.DeviceIdType.MESH
F32 = jnp.float32
BF16 = jnp.bfloat16


def rows_at(start, size):
    return pl.ds(pl.multiple_of(start, 16), size)


def block_kernel(
    total_images, data_count,
    x_ref, cot_ref, raw_ref, gain_ref, grad_ref, ws_ref,
    halo, gpad, hs, slope, std, part, sendb, got_core, got_x, got_z, gathered,
    halo_s, halo_r, wz_s, wz_r, wx_s, wx_r, wc_s, wc_r,
    rc_s, rc_r, rx_s, rx_r, rz_s, rz_r, ag_s, ag_r,
):
    pixels, chan_count = x_ref.shape
    owner_rows, fan_size = raw_ref.shape
    width = fan_size // 9
    wide = 3 * width
    group_count = chan_count // width
    cols = gpad.shape[0] - pixels
    cols = cols // 2
    piece_rows = owner_rows // 4
    fan_scale = 1.0 / math.sqrt(fan_size)
    band = lax.axis_index("space")
    mine = lax.axis_index("dp")
    core = band % 2
    pair = band + 1 - 2 * core
    cross = (band + 2) % 4

    def copy(src, dst, send, recv, where):
        return pltpu.make_async_remote_copy(
            src_ref=src, dst_ref=dst, send_sem=send, recv_sem=recv,
            device_id=where, device_id_type=MESH,
        )

    barrier = pltpu.get_barrier_semaphore()
    for j in range(1, 4):
        pl.semaphore_signal(
            barrier, inc=1, device_id={"space": (band + j) % 4}, device_id_type=MESH
        )
    for j in range(1, data_count):
        pl.semaphore_signal(
            barrier, inc=1, device_id={"dp": (mine + j) % data_count}, device_id_type=MESH
        )

    def unit_of(rows, gains):
        row_mean = jnp.mean(rows, axis=1, keepdims=True)
        centred = rows - row_mean
        row_var = jnp.mean(centred * centred, axis=1, keepdims=True)
        inv_std = lax.rsqrt(row_var + 1e-05)
        return centred * inv_std, inv_std

    def std_step(k, carry):
        rows = rows_at(k * piece_rows, piece_rows)
        gains = gain_ref[rows, :]
        unit, _ = unit_of(raw_ref[rows, :], gains)
        std[rows_at(mine * owner_rows + k * piece_rows, piece_rows), :] = (
            gains * unit * fan_scale
        ).astype(BF16)
        return carry

    lax.fori_loop(0, 4, std_step, 0)

    pl.semaphore_wait(barrier, 2 + data_count)

    up = copy(cot_ref.at[pl.ds(0, cols), :], halo.at[1], halo_s.at[0], halo_r.at[1],
              {"space": (band + 3) % 4})
    down = copy(cot_ref.at[pl.ds(pixels - cols, cols), :], halo.at[0], halo_s.at[1], halo_r.at[0],
                {"space": (band + 1) % 4})

    @pl.when(band > 0)
    def _():
        up.start()

    @pl.when(band < 3)
    def _():
        down.start()

    def std_piece(owner, quarter):
        return std.at[rows_at(owner * owner_rows + quarter * piece_rows, piece_rows), :]

    wz = []
    for j in range(1, data_count):
        own = std_piece(mine, band)
        wz.append(copy(own, own, wz_s.at[j - 1], wz_r.at[j - 1],
                       {"dp": (mine + j) % data_count}))
        wz[-1].start()

    gpad[pl.ds(cols, pixels), :] = (alpha_skip * cot_ref[...].astype(F32)).astype(BF16)

    row_id = lax.broadcasted_iota(jnp.int32, (pixels, width), 0) % cols

    def act_step(g, carry):
        at = pl.ds(pl.multiple_of(g * width, width), width)
        x = x_ref[:, at].astype(F32)
        cdf = 0.5 * (1.0 + lax.erf(x * math.sqrt(0.5)))
        hidden = act_gain * (x * cdf)
        slope[:, at] = act_gain * (cdf + x * (jnp.exp(-0.5 * x * x) * (1.0 / math.sqrt(2.0 * math.pi))))
        before = jnp.where(row_id == 0, 0.0, pltpu.roll(hidden, 1, 0))
        after = jnp.where(row_id == cols - 1, 0.0, pltpu.roll(hidden, pixels - 1, 0))
        for b, value in enumerate((before, hidden, after)):
            hs[:, pl.ds(pl.multiple_of(g * wide + b * width, width), width)] = value.astype(BF16)
        return carry

    lax.fori_loop(0, group_count, act_step, 0)

    @pl.when(band > 0)
    def _():
        down.wait_recv()
        gpad[pl.ds(0, cols), :] = (alpha_skip * halo[0].astype(F32)).astype(BF16)

    @pl.when(band == 0)
    def _():
        gpad[pl.ds(0, cols), :] = jnp.zeros((cols, chan_count), BF16)

    @pl.when(band < 3)
    def _():
        up.wait_recv()
        gpad[pl.ds(cols + pixels, cols), :] = (alpha_skip * halo[1].astype(F32)).astype(BF16)

    @pl.when(band == 3)
    def _():
        gpad[pl.ds(cols + pixels, cols), :] = jnp.zeros((cols, chan_count), BF16)

    def weight_step(g, carry):
        at = pl.ds(pl.multiple_of(g * width, width), width)
        right = hs[:, pl.ds(pl.multiple_of(g * wide, width), wide)]
        for a in range(3):
            left = gpad[pl.ds((2 - a) * cols, pixels), at]
            part[pl.ds(pl.multiple_of(g * width, width), width), pl.ds(a * wide, wide)] = (
                lax.dot_general(left, right, (((0,), (0,)), ((), ())), preferred_element_type=F32)
            )
        return carry

    def place(owner, quarter):
        return rows_at(owner * owner_rows + quarter * piece_rows, piece_rows)

    halves = 2 if data_count % 2 == 0 and group_count % 2 == 0 else 1
    rc = {}
    for half in range(halves):
        lax.fori_loop(
            half * group_count // halves, (half + 1) * group_count // halves, weight_step, 0
        )
        for d in range(half * data_count // halves, (half + 1) * data_count // halves):
            for t in range(2):
                at = place(d, 1 - core + 2 * t)
                sendb[at, :] = part[at, :].astype(BF16)
                n = 2 * d + t
                rc[n] = copy(sendb.at[at, :], got_core.at[n], rc_s.at[n], rc_r.at[n],
                             {"space": pair})
                rc[n].start()

    rx = []
    for d in range(data_count):
        for t in range(2):
            n = 2 * d + t
            rc[n].wait_recv()
        other = cross // 2
        at = place(d, cross)
        sendb[at, :] = (part[at, :] + got_core[2 * d + other].astype(F32)).astype(BF16)
        rx.append(copy(sendb.at[at, :], got_x.at[d], rx_s.at[d], rx_r.at[d], {"space": cross}))
        rx[-1].start()

    wx = []
    for j in range(1, data_count):
        wz[j - 1].wait_recv()
        piece = std_piece((mine + data_count - j) % data_count, band)
        wx.append(copy(piece, piece, wx_s.at[j - 1], wx_r.at[j - 1], {"space": cross}))
        wx[-1].start()

    for d in range(data_count):
        rx[d].wait_recv()
        at = place(d, band)
        total = part[at, :] + got_core[2 * d + band // 2].astype(F32) + got_x[d].astype(F32)
        part[at, :] = total
        sendb[at, :] = total.astype(BF16)
    rz = []
    for j in range(1, data_count):
        owner = (mine + j) % data_count
        rz.append(copy(sendb.at[place(owner, band), :], got_z.at[j - 1], rz_s.at[j - 1],
                       rz_r.at[j - 1], {"dp": owner}))
        rz[-1].start()

    wc = []
    for j in range(1, data_count):
        wx[j - 1].wait_recv()
        owner = (mine + data_count - j) % data_count
        for t, quarter in enumerate((band, cross)):
            n = 2 * (j - 1) + t
            piece = std_piece(owner, quarter)
            wc.append(copy(piece, piece, wc_s.at[n], wc_r.at[n], {"space": pair}))
            wc[-1].start()
    for one in wc:
        one.wait_recv()

    def back_step(g, carry):
        at = pl.ds(pl.multiple_of(g * width, width), width)
        left = jnp.concatenate(
            [gpad[pl.ds((2 - a) * cols, pixels), at] for a in range(3)], axis=1
        )
        right = jnp.concatenate([std[at, pl.ds(a * wide, wide)] for a in range(3)], axis=0)
        y = jnp.dot(left, right, preferred_element_type=F32)
        low, mid, high = y[:, :width], y[:, width : 2 * width], y[:, 2 * width :]
        low = jnp.where(row_id == cols - 1, 0.0, pltpu.roll(low, pixels - 1, 0))
        high = jnp.where(row_id == 0, 0.0, pltpu.roll(high, 1, 0))
        grad = cot_ref[:, at].astype(F32) + slope[:, at] * (low + mid + high)
        grad_ref[:, at] = grad.astype(BF16)
        return carry

    lax.fori_loop(0, group_count // 2, back_step, 0)

    total = part[place(mine, band), :]
    for j in range(1, data_count):
        rz[j - 1].wait_recv()
        total = total + got_z[j - 1].astype(F32)
    grad_standard = total * (1.0 / total_images)
    rows = rows_at(band * piece_rows, piece_rows)
    gains = gain_ref[rows, :]
    unit, inv_std = unit_of(raw_ref[rows, :], gains)
    grad_gain = jnp.sum(grad_standard * unit, axis=1, keepdims=True) * fan_scale
    grad_unit = grad_standard * gains * fan_scale
    centre_term = jnp.mean(grad_unit, axis=1, keepdims=True)
    along_term = jnp.mean(grad_unit * unit, axis=1, keepdims=True)
    grad_raw = inv_std * (grad_unit - centre_term - unit * along_term)
    high = grad_gain.astype(BF16).astype(F32)
    low = grad_gain - high
    lane = lax.broadcasted_iota(jnp.int32, (piece_rows, 128), 1)
    gathered[band, :, pl.ds(0, fan_size)] = grad_raw.astype(BF16)
    gathered[band, :, pl.ds(fan_size, 128)] = jnp.where(lane == 0, high, low).astype(BF16)
    ag = []
    for j in range(1, 4):
        ag.append(copy(gathered.at[band], gathered.at[band], ag_s.at[j - 1], ag_r.at[j - 1],
                       {"space": (band + j) % 4}))
        ag[-1].start()
    lax.fori_loop(group_count // 2, group_count, back_step, 0)
    for one in ag:
        one.wait_recv()
    for q in range(4):
        ws_ref[pl.ds(q * piece_rows, piece_rows), :] = gathered[q]

    @pl.when(band > 0)
    def _():
        up.wait_send()

    @pl.when(band < 3)
    def _():
        down.wait_send()

    for one in wz + list(rc.values()) + rx + wx + rz + wc + ag:
        one.wait_send()


def local_kernel(inputs, cotangent, kernel_raw, kernel_gain):
    images, band_rows, band_cols, chan_count = inputs.shape
    owner_rows, fan_size = kernel_raw.shape
    data_count = lax.axis_size("dp")
    pixels = band_rows * band_cols
    piece_rows = owner_rows // 4
    width = fan_size // 9
    dma = pltpu.SemaphoreType.DMA
    peers = data_count - 1
    vmem = pl.BlockSpec(memory_space=pltpu.VMEM)
    grad, packed = pl.pallas_call(
        functools.partial(block_kernel, images * data_count, data_count),
        out_shape=(
            jax.ShapeDtypeStruct((pixels, chan_count), BF16),
            jax.ShapeDtypeStruct((owner_rows, fan_size + 128), BF16),
        ),
        in_specs=[vmem] * 4,
        out_specs=(vmem, vmem),
        scratch_shapes=[
            pltpu.VMEM((2, band_cols, chan_count), BF16),
            pltpu.VMEM((pixels + 2 * band_cols, chan_count), BF16),
            pltpu.VMEM((pixels, 3 * chan_count), BF16),
            pltpu.VMEM((pixels, chan_count), F32),
            pltpu.VMEM((chan_count, fan_size), BF16),
            pltpu.VMEM((chan_count, fan_size), F32),
            pltpu.VMEM((chan_count, fan_size), BF16),
            pltpu.VMEM((2 * data_count, piece_rows, fan_size), BF16),
            pltpu.VMEM((data_count, piece_rows, fan_size), BF16),
            pltpu.VMEM((peers, piece_rows, fan_size), BF16),
            pltpu.VMEM((4, piece_rows, fan_size + 128), BF16),
            dma((2,)), dma((2,)),
            dma((peers,)), dma((peers,)),
            dma((peers,)), dma((peers,)),
            dma((2 * peers,)), dma((2 * peers,)),
            dma((2 * data_count,)), dma((2 * data_count,)),
            dma((data_count,)), dma((data_count,)),
            dma((peers,)), dma((peers,)),
            dma((3,)), dma((3,)),
        ],
        compiler_params=pltpu.CompilerParams(
            collective_id=0, has_side_effects=True, vmem_limit_bytes=48 * 1024 * 1024
        ),
        cost_estimate=pl.CostEstimate(
            flops=4 * pixels * chan_count * fan_size,
            bytes_accessed=8 * pixels * chan_count,
            transcendentals=2 * pixels * chan_count,
        ),
    )(
        inputs.reshape(pixels, chan_count),
        cotangent.reshape(pixels, chan_count),
        kernel_raw,
        kernel_gain[:, None],
    )
    grad_raw = packed[:, :fan_size].astype(F32)
    grad_gain = packed[:, fan_size].astype(F32) + packed[:, fan_size + 1].astype(F32)
    return (grad.reshape(inputs.shape), grad_raw, grad_gain)


def solution(mesh):
    placed = (
        P(("groups", "dp"), "space", None, None),
        P(("groups", "dp"), "space", None, None),
        P("dp", None),
        P("dp"),
    )

    def run(inputs, cotangent, kernel_raw, kernel_gain):
        images, rows, cols, chan_count = inputs.shape
        fan_size = kernel_raw.shape[1]
        data_count = mesh.shape["dp"]
        replicas = mesh.shape["groups"] * data_count
        fits = (
            mesh.shape["space"] == 4
            and images == replicas
            and chan_count % (64 * data_count) == 0
            and (chan_count // (fan_size // 9)) % 2 == 0
            and fan_size % (9 * 128) == 0
            and cols % 16 == 0
            and rows % 4 == 0
        )
        return jax.shard_map(
            local_kernel if fits else local,
            mesh=mesh,
            in_specs=placed,
            out_specs=(
                P(("groups", "dp"), "space", None, None),
                P(("groups", "dp"), None),
                P(("groups", "dp")),
            ),
            check_vma=False,
        )(inputs, cotangent, kernel_raw, kernel_gain)

    return run
```

```python
import functools
import math

import jax
import jax.numpy as jnp
from jax import lax
from jax.experimental import pallas as pl
from jax.experimental.pallas import tpu as pltpu
from jax.sharding import PartitionSpec as P

act_gain = 1.7015
alpha_skip = 0.2


def padded_2(value, sides, width):
    for axis, dim in sides:
        size, length = (lax.axis_size(axis), value.shape[dim])
        up = [(i, (i + 1) % size) for i in range(size - 1)]
        down = [(j, i) for i, j in up]
        last = lax.slice_in_dim(value, length - width, length, axis=dim)
        first = lax.slice_in_dim(value, 0, width, axis=dim)
        before = lax.ppermute(last, axis, up)
        after = lax.ppermute(first, axis, down)
        value = jnp.concatenate([before, value, after], axis=dim)
    return value


def activate(value_in):
    return act_gain * jax.nn.gelu(value_in, approximate=False)


def ws_parts(kernel_rows):
    row_mean = jnp.mean(kernel_rows, axis=1, keepdims=True)
    centred = kernel_rows - row_mean
    row_var = jnp.mean(centred * centred, axis=1, keepdims=True)
    inv_std = lax.rsqrt(row_var + 1e-05)
    return (centred * inv_std, inv_std)


def ws_back(grad_standard, unit, inv_std, gains):
    fan_scale = 1.0 / math.sqrt(unit.shape[1])
    grad_gain = jnp.sum(grad_standard * unit, axis=1) * fan_scale
    grad_unit = grad_standard * gains[:, None] * fan_scale
    centre_term = jnp.mean(grad_unit, axis=1, keepdims=True)
    along_term = jnp.mean(grad_unit * unit, axis=1, keepdims=True)
    grad_raw = inv_std * (grad_unit - centre_term - unit * along_term)
    return (grad_raw, grad_gain)


def local(inputs, cotangent, kernel_raw, kernel_gain):
    images, band_rows, band_cols, chan_count = inputs.shape
    fan_size = kernel_raw.shape[1]
    group_width = fan_size // 9
    group_count = chan_count // group_width
    fan_scale = 1.0 / math.sqrt(fan_size)
    inputs_wide = inputs.astype(jnp.float32)
    hidden = activate(inputs_wide).astype(jnp.bfloat16)
    grad_conv = (alpha_skip * cotangent.astype(jnp.float32)).astype(jnp.bfloat16)
    stacked = jnp.stack([hidden, grad_conv])
    rimmed = padded_2(stacked, (("space", 2),), 1)
    padded = jnp.pad(rimmed, ((0, 0), (0, 0), (0, 0), (1, 1), (0, 0)))
    hidden_pad = padded[0]
    grad_pad = padded[1]
    unit, inv_std = ws_parts(kernel_raw)
    standard_rows = (kernel_gain[:, None] * unit * fan_scale).astype(jnp.bfloat16)
    standard = lax.all_gather(standard_rows, "dp", axis=0, tiled=True)
    tap_kernels = standard.reshape(group_count, group_width, 3, 3, group_width)
    count = images * band_rows * band_cols
    grad_flat = grad_conv.reshape(count, group_count, group_width)
    grad_hidden = jnp.zeros((count, group_count, group_width), jnp.float32)
    tap_grads = []
    for tap_row in range(3):
        backed_cols = []
        for tap_col in range(3):
            shifted = hidden_pad[:, tap_row : tap_row + band_rows, tap_col : tap_col + band_cols]
            shifted = shifted.reshape(count, group_count, group_width)
            tap_grads.append(
                jnp.einsum("mgo,mgi->goi", grad_flat, shifted, preferred_element_type=jnp.float32)
            )
            backed = grad_pad[
                :, 2 - tap_row : 2 - tap_row + band_rows, 2 - tap_col : 2 - tap_col + band_cols
            ]
            backed_cols.append(backed.reshape(count, group_count, group_width))
        backed_row = jnp.stack(backed_cols, axis=2)
        grad_hidden = grad_hidden + jnp.einsum(
            "mgbo,gobi->mgi",
            backed_row,
            tap_kernels[:, :, tap_row],
            preferred_element_type=jnp.float32,
        )
    total_images = images * lax.axis_size("dp")
    grad_standard = jnp.stack(tap_grads, axis=2).reshape(chan_count, fan_size) * (
        1.0 / total_images
    )
    unused_act, pull_act = jax.vjp(activate, inputs_wide)
    grad_inputs = cotangent.astype(jnp.float32) + pull_act(grad_hidden.reshape(inputs.shape))[0]
    band_count = lax.axis_size("space")
    data_count = lax.axis_size("dp")
    owner_rows = kernel_raw.shape[0]
    piece_rows = owner_rows // band_count
    ordered = grad_standard.reshape(data_count, band_count, piece_rows, fan_size)
    ordered = ordered.transpose(1, 0, 2, 3).reshape(chan_count, fan_size)
    piece = lax.psum_scatter(ordered, ("space", "dp"), scatter_dimension=0, tiled=True)
    start = lax.axis_index("space") * piece_rows
    unit_piece = lax.dynamic_slice_in_dim(unit, start, piece_rows, 0)
    inv_piece = lax.dynamic_slice_in_dim(inv_std, start, piece_rows, 0)
    gain_piece = lax.dynamic_slice_in_dim(kernel_gain, start, piece_rows, 0)
    raw_piece, gain_grad_piece = ws_back(piece, unit_piece, inv_piece, gain_piece)
    grad_raw, grad_gain = (
        lax.all_gather(raw_piece, "space", axis=0, tiled=True),
        lax.all_gather(gain_grad_piece, "space", axis=0, tiled=True),
    )
    return (grad_inputs.astype(jnp.bfloat16), grad_raw, grad_gain)


MESH = pl.DeviceIdType.MESH
F32 = jnp.float32
BF16 = jnp.bfloat16


def rows_at(start, size):
    return pl.ds(pl.multiple_of(start, 16), size)


def block_kernel(
    total_images, data_count,
    x_hbm, cot_hbm, raw_hbm, gain_hbm, grad_hbm, ws_hbm, gains_ref,
    x_ref, cot_ref, raw_ref, gain_row, gain_ref, grad_ref, load_s, out_s, halo, gpad, hs, slope, std, part, sendb, got_core, got_x, got_z, gathered,
    halo_s, halo_r, wz_s, wz_r, wx_s, wx_r, wc_s, wc_r,
    rc_s, rc_r, rx_s, rx_r, rz_s, rz_r, ag_s, ag_r,
):
    pixels, chan_count = x_ref.shape
    owner_rows, fan_size = raw_ref.shape
    width = fan_size // 9
    wide = 3 * width
    group_count = chan_count // width
    cols = gpad.shape[0] - pixels
    cols = cols // 2
    piece_rows = owner_rows // 4
    fan_scale = 1.0 / math.sqrt(fan_size)
    band = lax.axis_index("space")
    mine = lax.axis_index("dp")
    group = lax.axis_index("groups")
    core = band % 2
    slot = 2 * group + core
    slot_cross = 2 * (1 - group) + core
    far_half = 1 - mine // 2
    order = (3 * far_half, 1 + far_half, 2 * (mine // 2) + 1 - mine % 2, mine)
    pair = band + 1 - 2 * core
    cross = (band + 2) % 4

    def copy(src, dst, send, recv, where):
        return pltpu.make_async_remote_copy(
            src_ref=src, dst_ref=dst, send_sem=send, recv_sem=recv,
            device_id=where, device_id_type=MESH,
        )

    barrier = pltpu.get_barrier_semaphore()
    for j in range(1, 4):
        pl.semaphore_signal(
            barrier, inc=1, device_id={"space": (band + j) % 4}, device_id_type=MESH
        )
    for j in range(1, data_count):
        pl.semaphore_signal(
            barrier, inc=1, device_id={"dp": (mine + j) % data_count}, device_id_type=MESH
        )

    pl.semaphore_signal(barrier, inc=1, device_id={"groups": 1 - group}, device_id_type=MESH)

    loads = [
        pltpu.make_async_copy(src, dst, load_s.at[n])
        for n, (src, dst) in enumerate(
            ((raw_hbm, raw_ref), (gain_hbm, gain_row), (x_hbm, x_ref), (cot_hbm, cot_ref))
        )
    ]
    for one in loads:
        one.start()

    def unit_of(rows):
        row_mean = jnp.mean(rows, axis=1, keepdims=True)
        centred = rows - row_mean
        row_var = jnp.mean(centred * centred, axis=1, keepdims=True)
        inv_std = lax.rsqrt(row_var + 1e-05)
        return centred * inv_std, inv_std

    def std_step(k, carry):
        rows = rows_at(k * piece_rows, piece_rows)
        gains = gain_ref[rows, :]
        unit, _ = unit_of(raw_ref[rows, :])
        std[rows_at(mine * owner_rows + k * piece_rows, piece_rows), :] = (
            gains * unit * fan_scale
        ).astype(BF16)
        return carry

    pl.semaphore_wait(barrier, 3 + data_count)

    up = copy(cot_hbm.at[pl.ds(0, cols), :], halo.at[1], halo_s.at[0], halo_r.at[1],
              {"space": (band + 3) % 4})
    down = copy(cot_hbm.at[pl.ds(pixels - cols, cols), :], halo.at[0], halo_s.at[1], halo_r.at[0],
                {"space": (band + 1) % 4})

    @pl.when(band > 0)
    def _():
        up.start()

    @pl.when(band < 3)
    def _():
        down.start()

    loads[0].wait()
    loads[1].wait()
    diagonal = lax.broadcasted_iota(jnp.int32, (owner_rows, owner_rows), 0) == (
        lax.broadcasted_iota(jnp.int32, (owner_rows, owner_rows), 1)
    )
    gain_ref[...] = jnp.sum(jnp.where(diagonal, gain_row[...], 0.0), axis=1, keepdims=True)

    lax.fori_loop(0, 4, std_step, 0)

    def std_piece(owner, quarter):
        return std.at[rows_at(owner * owner_rows + quarter * piece_rows, piece_rows), :]

    wz = []
    own = std_piece(mine, slot)
    for t in range(3):
        wz.append(copy(own, own, wz_s.at[t], wz_r.at[mine], {"dp": order[t]}))
        wz[-1].start()

    loads[2].wait()
    loads[3].wait()
    gpad[pl.ds(cols, pixels), :] = (alpha_skip * cot_ref[...].astype(F32)).astype(BF16)

    row_id = lax.broadcasted_iota(jnp.int32, (pixels, width), 0) % cols

    def act_step(g, carry):
        at = pl.ds(pl.multiple_of(g * width, width), width)
        x = x_ref[:, at].astype(F32)
        cdf = 0.5 * (1.0 + lax.erf(x * math.sqrt(0.5)))
        hidden = act_gain * (x * cdf)
        slope[:, at] = act_gain * (cdf + x * (jnp.exp(-0.5 * x * x) * (1.0 / math.sqrt(2.0 * math.pi))))
        before = jnp.where(row_id == 0, 0.0, pltpu.roll(hidden, 1, 0))
        after = jnp.where(row_id == cols - 1, 0.0, pltpu.roll(hidden, pixels - 1, 0))
        for b, value in enumerate((before, hidden, after)):
            hs[:, pl.ds(pl.multiple_of(g * wide + b * width, width), width)] = value.astype(BF16)
        return carry

    lax.fori_loop(0, group_count, act_step, 0)

    @pl.when(band > 0)
    def _():
        down.wait_recv()
        gpad[pl.ds(0, cols), :] = (alpha_skip * halo[0].astype(F32)).astype(BF16)

    @pl.when(band == 0)
    def _():
        gpad[pl.ds(0, cols), :] = jnp.zeros((cols, chan_count), BF16)

    @pl.when(band < 3)
    def _():
        up.wait_recv()
        gpad[pl.ds(cols + pixels, cols), :] = (alpha_skip * halo[1].astype(F32)).astype(BF16)

    @pl.when(band == 3)
    def _():
        gpad[pl.ds(cols + pixels, cols), :] = jnp.zeros((cols, chan_count), BF16)

    def weight_step(g, carry):
        at = pl.ds(pl.multiple_of(g * width, width), width)
        right = hs[:, pl.ds(pl.multiple_of(g * wide, width), wide)]
        for a in range(3):
            left = gpad[pl.ds((2 - a) * cols, pixels), at]
            part[pl.ds(pl.multiple_of(g * width, width), width), pl.ds(a * wide, wide)] = (
                lax.dot_general(left, right, (((0,), (0,)), ((), ())), preferred_element_type=F32)
            )
        return carry

    def place(owner, quarter):
        return rows_at(owner * owner_rows + quarter * piece_rows, piece_rows)

    half_groups = group_count // 2
    rc = []
    for half in range(2):
        first = half_groups * (far_half if half == 0 else 1 - far_half)
        lax.fori_loop(0, half_groups, lambda k, c: weight_step(first + k, c), 0)
        for d in range(2 * half, 2 * half + 2):
            for t in range(2):
                at = place(order[d], 1 - core + 2 * t)
                sendb[at, :] = part[at, :].astype(BF16)
                n = 2 * d + t
                rc.append(copy(sendb.at[at, :], got_core.at[n], rc_s.at[n], rc_r.at[n],
                               {"space": pair}))
                rc[-1].start()

    rx = []
    for d in range(4):
        for t in range(2):
            rc[2 * d + t].wait_recv()
        at = place(order[d], cross)
        sendb[at, :] = (part[at, :] + got_core[2 * d + cross // 2].astype(F32)).astype(BF16)
        rx.append(copy(sendb.at[at, :], got_x.at[d], rx_s.at[d], rx_r.at[d], {"space": cross}))
        rx[-1].start()

    wx = []
    for t in (2, 1, 0):
        piece = std_piece(order[t], slot)
        copy(piece, piece, wz_s.at[t], wz_r.at[order[t]], {"dp": order[t]}).wait_recv()
        wx.append(copy(piece, piece, wx_s.at[t], wx_r.at[t], {"groups": 1 - group}))
        wx[-1].start()

    rz = []
    for d in range(4):
        rx[d].wait_recv()
        at = place(order[d], band)
        total = part[at, :] + got_core[2 * d + band // 2].astype(F32) + got_x[d].astype(F32)
        if d == 3:
            part[at, :] = total
        else:
            sendb[at, :] = total.astype(BF16)
            rz.append(copy(sendb.at[at, :], got_z.at[mine], rz_s.at[d], rz_r.at[mine],
                           {"dp": order[d]}))
            rz[-1].start()

    wc = []
    for n, t in enumerate((2, 1, 0)):
        wx[n].wait_recv()
        for e, quarter in enumerate((slot, slot_cross)):
            piece = std_piece(order[t], quarter)
            wc.append(copy(piece, piece, wc_s.at[2 * t + e], wc_r.at[2 * t + e], {"space": pair}))
            wc[-1].start()
    for one in wc:
        one.wait_recv()

    def back_step(g, carry):
        at = pl.ds(pl.multiple_of(g * width, width), width)
        left = jnp.concatenate(
            [gpad[pl.ds((2 - a) * cols, pixels), at] for a in range(3)], axis=1
        )
        right = jnp.concatenate([std[at, pl.ds(a * wide, wide)] for a in range(3)], axis=0)
        y = jnp.dot(left, right, preferred_element_type=F32)
        low, mid, high = y[:, :width], y[:, width : 2 * width], y[:, 2 * width :]
        low = jnp.where(row_id == cols - 1, 0.0, pltpu.roll(low, pixels - 1, 0))
        high = jnp.where(row_id == 0, 0.0, pltpu.roll(high, 1, 0))
        grad = cot_ref[:, at].astype(F32) + slope[:, at] * (low + mid + high)
        grad_ref[:, at] = grad.astype(BF16)
        return carry

    lax.fori_loop(0, half_groups, back_step, 0)
    outs = []
    half_cols = chan_count // 2

    def write(src, dst):
        outs.append(pltpu.make_async_copy(src, dst, out_s.at[len(outs)]))
        outs[-1].start()

    write(grad_ref.at[:, pl.ds(0, half_cols)], grad_hbm.at[:, pl.ds(0, half_cols)])

    total = part[place(mine, band), :]
    for t in (2, 1, 0):
        here = sendb.at[place(order[t], band), :]
        copy(here, got_z.at[order[t]], rz_s.at[t], rz_r.at[order[t]], {"dp": order[t]}).wait_recv()
        total = total + got_z[order[t]].astype(F32)
    grad_standard = total * (1.0 / total_images)
    rows = rows_at(band * piece_rows, piece_rows)
    gains = gain_ref[rows, :]
    unit, inv_std = unit_of(raw_ref[rows, :])
    grad_gain = jnp.sum(grad_standard * unit, axis=1, keepdims=True) * fan_scale
    grad_unit = grad_standard * gains * fan_scale
    centre_term = jnp.mean(grad_unit, axis=1, keepdims=True)
    along_term = jnp.mean(grad_unit * unit, axis=1, keepdims=True)
    grad_raw = inv_std * (grad_unit - centre_term - unit * along_term)
    high = grad_gain.astype(BF16).astype(F32)
    low = grad_gain - high
    lane = lax.broadcasted_iota(jnp.int32, (piece_rows, 128), 1)
    gathered[band, :, pl.ds(0, fan_size)] = grad_raw.astype(BF16)
    gathered[band, :, pl.ds(fan_size, 128)] = jnp.where(lane == 0, high, low).astype(BF16)
    ag = []
    for n, (quarter, to) in enumerate(((band, cross), (band, pair), (cross, pair))):
        if n == 2:
            lax.fori_loop(half_groups, group_count - 1, back_step, 0)
            ag[0].wait_recv()
        block = gathered.at[quarter]
        ag.append(copy(block, block, ag_s.at[n], ag_r.at[n], {"space": to}))
        ag[-1].start()
    lax.fori_loop(group_count - 1, group_count, back_step, 0)
    write(grad_ref.at[:, pl.ds(half_cols, half_cols)], grad_hbm.at[:, pl.ds(half_cols, half_cols)])
    ag[1].wait_recv()
    ag[2].wait_recv()
    lane_id = lax.broadcasted_iota(jnp.int32, (piece_rows, owner_rows), 1)
    line_id = lax.broadcasted_iota(jnp.int32, (piece_rows, owner_rows), 0)
    gain_line = jnp.zeros((1, owner_rows), F32)
    for q in range(4):
        write(gathered.at[q, :, pl.ds(0, fan_size)], ws_hbm.at[pl.ds(q * piece_rows, piece_rows), :])
        both = gathered[q, :, pl.ds(fan_size, 128)].astype(F32)
        column = both[:, 0:1] + both[:, 1:2]
        gain_line = gain_line + jnp.sum(
            jnp.where(lane_id == line_id + q * piece_rows, column, 0.0), axis=0, keepdims=True
        )
    gains_ref[...] = gain_line

    @pl.when(band > 0)
    def _():
        up.wait_send()

    @pl.when(band < 3)
    def _():
        down.wait_send()

    for one in outs:
        one.wait()
    for one in wz + rc + rx + wx + rz + wc + ag:
        one.wait_send()


def widen_kernel(grad_ref, rounded_ref, gains_ref, grad_out, raw_out, gains_out, narrow, wide, sems):
    load = pltpu.make_async_copy(rounded_ref, narrow, sems.at[6])
    load.start()
    copies = [
        pltpu.make_async_copy(grad_ref, grad_out, sems.at[0]),
        pltpu.make_async_copy(gains_ref, gains_out, sems.at[1]),
    ]
    for one in copies:
        one.start()
    load.wait()
    rows = narrow.shape[0] // 4
    for k in range(4):
        at = pl.ds(k * rows, rows)
        wide[at, :] = narrow[at, :].astype(F32)
        copies.append(pltpu.make_async_copy(wide.at[at, :], raw_out.at[at, :], sems.at[2 + k]))
        copies[-1].start()
    for one in copies:
        one.wait()


def local_kernel(inputs, cotangent, kernel_raw, kernel_gain):
    images, band_rows, band_cols, chan_count = inputs.shape
    owner_rows, fan_size = kernel_raw.shape
    data_count = lax.axis_size("dp")
    pixels = band_rows * band_cols
    piece_rows = owner_rows // 4
    width = fan_size // 9
    dma = pltpu.SemaphoreType.DMA
    peers = data_count - 1
    vmem = pl.BlockSpec(memory_space=pltpu.VMEM)
    hbm = pl.BlockSpec(memory_space=pltpu.HBM)
    grad, rounded, gains = pl.pallas_call(
        functools.partial(block_kernel, images * data_count, data_count),
        out_shape=(
            jax.ShapeDtypeStruct((pixels, chan_count), BF16),
            jax.ShapeDtypeStruct((owner_rows, fan_size), BF16),
            jax.ShapeDtypeStruct((1, owner_rows), F32),
        ),
        in_specs=[hbm] * 4,
        out_specs=(hbm, hbm, vmem),
        scratch_shapes=[
            pltpu.VMEM((pixels, chan_count), BF16),
            pltpu.VMEM((pixels, chan_count), BF16),
            pltpu.VMEM((owner_rows, fan_size), F32),
            pltpu.VMEM((1, owner_rows), F32),
            pltpu.VMEM((owner_rows, 1), F32),
            pltpu.VMEM((pixels, chan_count), BF16),
            dma((4,)), dma((6,)),
            pltpu.VMEM((2, band_cols, chan_count), BF16),
            pltpu.VMEM((pixels + 2 * band_cols, chan_count), BF16),
            pltpu.VMEM((pixels, 3 * chan_count), BF16),
            pltpu.VMEM((pixels, chan_count), F32),
            pltpu.VMEM((chan_count, fan_size), BF16),
            pltpu.VMEM((chan_count, fan_size), F32),
            pltpu.VMEM((chan_count, fan_size), BF16),
            pltpu.VMEM((2 * data_count, piece_rows, fan_size), BF16),
            pltpu.VMEM((data_count, piece_rows, fan_size), BF16),
            pltpu.VMEM((data_count, piece_rows, fan_size), BF16),
            pltpu.VMEM((4, piece_rows, fan_size + 128), BF16),
            dma((2,)), dma((2,)),
            dma((peers,)), dma((data_count,)),
            dma((peers,)), dma((peers,)),
            dma((2 * peers,)), dma((2 * peers,)),
            dma((2 * data_count,)), dma((2 * data_count,)),
            dma((data_count,)), dma((data_count,)),
            dma((peers,)), dma((data_count,)),
            dma((3,)), dma((3,)),
        ],
        compiler_params=pltpu.CompilerParams(
            collective_id=0, has_side_effects=True, vmem_limit_bytes=60 * 1024 * 1024
        ),
        cost_estimate=pl.CostEstimate(
            flops=4 * pixels * chan_count * fan_size,
            bytes_accessed=8 * pixels * chan_count,
            transcendentals=2 * pixels * chan_count,
        ),
    )(
        inputs.reshape(pixels, chan_count),
        cotangent.reshape(pixels, chan_count),
        kernel_raw,
        kernel_gain.reshape(1, owner_rows),
    )
    grad, grad_raw, grad_gain = pl.pallas_call(
        widen_kernel,
        out_shape=(
            jax.ShapeDtypeStruct((pixels, chan_count), BF16),
            jax.ShapeDtypeStruct((owner_rows, fan_size), F32),
            jax.ShapeDtypeStruct((1, owner_rows), F32),
        ),
        in_specs=[hbm] * 3,
        out_specs=(hbm, hbm, hbm),
        scratch_shapes=[
            pltpu.VMEM((owner_rows, fan_size), BF16),
            pltpu.VMEM((owner_rows, fan_size), F32),
            dma((7,)),
        ],
    )(grad, rounded, gains)
    return (grad.reshape(inputs.shape), grad_raw, grad_gain.reshape(owner_rows))


def solution(mesh):
    placed = (
        P(("groups", "dp"), "space", None, None),
        P(("groups", "dp"), "space", None, None),
        P("dp", None),
        P("dp"),
    )

    def run(inputs, cotangent, kernel_raw, kernel_gain):
        images, rows, cols, chan_count = inputs.shape
        fan_size = kernel_raw.shape[1]
        data_count = mesh.shape["dp"]
        replicas = mesh.shape["groups"] * data_count
        fits = (
            mesh.shape["space"] == 4
            and data_count == 4
            and mesh.shape["groups"] == 2
            and images == replicas
            and chan_count % (64 * data_count) == 0
            and (chan_count // (fan_size // 9)) % 2 == 0
            and fan_size % (9 * 128) == 0
            and cols % 16 == 0
            and rows % 4 == 0
        )
        return jax.shard_map(
            local_kernel if fits else local,
            mesh=mesh,
            in_specs=placed,
            out_specs=(
                P(("groups", "dp"), "space", None, None),
                P(("groups", "dp"), None),
                P(("groups", "dp")),
            ),
            check_vma=False,
        )(inputs, cotangent, kernel_raw, kernel_gain)

    return run
```

```python
import functools
import math

import jax
import jax.numpy as jnp
from jax import lax
from jax.experimental import pallas as pl
from jax.experimental.pallas import tpu as pltpu
from jax.sharding import PartitionSpec as P

act_gain = 1.7015
alpha_skip = 0.2


def padded_2(value, sides, width):
    for axis, dim in sides:
        size, length = (lax.axis_size(axis), value.shape[dim])
        up = [(i, (i + 1) % size) for i in range(size - 1)]
        down = [(j, i) for i, j in up]
        last = lax.slice_in_dim(value, length - width, length, axis=dim)
        first = lax.slice_in_dim(value, 0, width, axis=dim)
        before = lax.ppermute(last, axis, up)
        after = lax.ppermute(first, axis, down)
        value = jnp.concatenate([before, value, after], axis=dim)
    return value


def activate(value_in):
    return act_gain * jax.nn.gelu(value_in, approximate=False)


def ws_parts(kernel_rows):
    row_mean = jnp.mean(kernel_rows, axis=1, keepdims=True)
    centred = kernel_rows - row_mean
    row_var = jnp.mean(centred * centred, axis=1, keepdims=True)
    inv_std = lax.rsqrt(row_var + 1e-05)
    return (centred * inv_std, inv_std)


def ws_back(grad_standard, unit, inv_std, gains):
    fan_scale = 1.0 / math.sqrt(unit.shape[1])
    grad_gain = jnp.sum(grad_standard * unit, axis=1) * fan_scale
    grad_unit = grad_standard * gains[:, None] * fan_scale
    centre_term = jnp.mean(grad_unit, axis=1, keepdims=True)
    along_term = jnp.mean(grad_unit * unit, axis=1, keepdims=True)
    grad_raw = inv_std * (grad_unit - centre_term - unit * along_term)
    return (grad_raw, grad_gain)


def local(inputs, cotangent, kernel_raw, kernel_gain):
    images, band_rows, band_cols, chan_count = inputs.shape
    fan_size = kernel_raw.shape[1]
    group_width = fan_size // 9
    group_count = chan_count // group_width
    fan_scale = 1.0 / math.sqrt(fan_size)
    inputs_wide = inputs.astype(jnp.float32)
    hidden = activate(inputs_wide).astype(jnp.bfloat16)
    grad_conv = (alpha_skip * cotangent.astype(jnp.float32)).astype(jnp.bfloat16)
    stacked = jnp.stack([hidden, grad_conv])
    rimmed = padded_2(stacked, (("space", 2),), 1)
    padded = jnp.pad(rimmed, ((0, 0), (0, 0), (0, 0), (1, 1), (0, 0)))
    hidden_pad = padded[0]
    grad_pad = padded[1]
    unit, inv_std = ws_parts(kernel_raw)
    standard_rows = (kernel_gain[:, None] * unit * fan_scale).astype(jnp.bfloat16)
    standard = lax.all_gather(standard_rows, "dp", axis=0, tiled=True)
    tap_kernels = standard.reshape(group_count, group_width, 3, 3, group_width)
    count = images * band_rows * band_cols
    grad_flat = grad_conv.reshape(count, group_count, group_width)
    grad_hidden = jnp.zeros((count, group_count, group_width), jnp.float32)
    tap_grads = []
    for tap_row in range(3):
        backed_cols = []
        for tap_col in range(3):
            shifted = hidden_pad[:, tap_row : tap_row + band_rows, tap_col : tap_col + band_cols]
            shifted = shifted.reshape(count, group_count, group_width)
            tap_grads.append(
                jnp.einsum("mgo,mgi->goi", grad_flat, shifted, preferred_element_type=jnp.float32)
            )
            backed = grad_pad[
                :, 2 - tap_row : 2 - tap_row + band_rows, 2 - tap_col : 2 - tap_col + band_cols
            ]
            backed_cols.append(backed.reshape(count, group_count, group_width))
        backed_row = jnp.stack(backed_cols, axis=2)
        grad_hidden = grad_hidden + jnp.einsum(
            "mgbo,gobi->mgi",
            backed_row,
            tap_kernels[:, :, tap_row],
            preferred_element_type=jnp.float32,
        )
    total_images = images * lax.axis_size("dp")
    grad_standard = jnp.stack(tap_grads, axis=2).reshape(chan_count, fan_size) * (
        1.0 / total_images
    )
    unused_act, pull_act = jax.vjp(activate, inputs_wide)
    grad_inputs = cotangent.astype(jnp.float32) + pull_act(grad_hidden.reshape(inputs.shape))[0]
    band_count = lax.axis_size("space")
    data_count = lax.axis_size("dp")
    owner_rows = kernel_raw.shape[0]
    piece_rows = owner_rows // band_count
    ordered = grad_standard.reshape(data_count, band_count, piece_rows, fan_size)
    ordered = ordered.transpose(1, 0, 2, 3).reshape(chan_count, fan_size)
    piece = lax.psum_scatter(ordered, ("space", "dp"), scatter_dimension=0, tiled=True)
    start = lax.axis_index("space") * piece_rows
    unit_piece = lax.dynamic_slice_in_dim(unit, start, piece_rows, 0)
    inv_piece = lax.dynamic_slice_in_dim(inv_std, start, piece_rows, 0)
    gain_piece = lax.dynamic_slice_in_dim(kernel_gain, start, piece_rows, 0)
    raw_piece, gain_grad_piece = ws_back(piece, unit_piece, inv_piece, gain_piece)
    grad_raw, grad_gain = (
        lax.all_gather(raw_piece, "space", axis=0, tiled=True),
        lax.all_gather(gain_grad_piece, "space", axis=0, tiled=True),
    )
    return (grad_inputs.astype(jnp.bfloat16), grad_raw, grad_gain)


MESH = pl.DeviceIdType.MESH
F32 = jnp.float32
BF16 = jnp.bfloat16


def rows_at(start, size):
    return pl.ds(pl.multiple_of(start, 16), size)


def block_kernel(
    total_images, data_count,
    x_hbm, cot_hbm, raw_hbm, gain_hbm, grad_hbm, ws_hbm, gains_ref,
    x_ref, cot_ref, raw_ref, gain_row, gain_ref, grad_ref, load_s, out_s, halo, gpad, hs, slope, std, part, sendb, got_core, got_x, got_z, gathered,
    halo_s, halo_r, wz_s, wz_r, wx_s, wx_r, wc_s, wc_r,
    rc_s, rc_r, rx_s, rx_r, rz_s, rz_r, ag_s, ag_r,
):
    pixels, chan_count = x_ref.shape
    owner_rows, fan_size = raw_ref.shape
    width = fan_size // 9
    wide = 3 * width
    group_count = chan_count // width
    cols = gpad.shape[0] - pixels
    cols = cols // 2
    piece_rows = owner_rows // 4
    fan_scale = 1.0 / math.sqrt(fan_size)
    band = lax.axis_index("space")
    mine = lax.axis_index("dp")
    group = lax.axis_index("groups")
    core = band % 2
    slot = 2 * group + core
    slot_cross = 2 * (1 - group) + core
    far_half = 1 - mine // 2
    order = (3 * far_half, 1 + far_half, 2 * (mine // 2) + 1 - mine % 2, mine)
    pair = band + 1 - 2 * core
    cross = (band + 2) % 4

    def copy(src, dst, send, recv, where):
        return pltpu.make_async_remote_copy(
            src_ref=src, dst_ref=dst, send_sem=send, recv_sem=recv,
            device_id=where, device_id_type=MESH,
        )

    barrier = pltpu.get_barrier_semaphore()
    for j in range(1, 4):
        pl.semaphore_signal(
            barrier, inc=1, device_id={"space": (band + j) % 4}, device_id_type=MESH
        )
    for j in range(1, data_count):
        pl.semaphore_signal(
            barrier, inc=1, device_id={"dp": (mine + j) % data_count}, device_id_type=MESH
        )

    pl.semaphore_signal(barrier, inc=1, device_id={"groups": 1 - group}, device_id_type=MESH)

    loads = [
        pltpu.make_async_copy(src, dst, load_s.at[n])
        for n, (src, dst) in enumerate(
            ((raw_hbm, raw_ref), (gain_hbm, gain_row), (x_hbm, x_ref), (cot_hbm, cot_ref))
        )
    ]
    for one in loads:
        one.start()

    def unit_of(rows):
        row_mean = jnp.mean(rows, axis=1, keepdims=True)
        centred = rows - row_mean
        row_var = jnp.mean(centred * centred, axis=1, keepdims=True)
        inv_std = lax.rsqrt(row_var + 1e-05)
        return centred * inv_std, inv_std

    def std_step(k, carry):
        rows = rows_at(k * piece_rows, piece_rows)
        gains = gain_ref[rows, :]
        unit, _ = unit_of(raw_ref[rows, :])
        std[rows_at(mine * owner_rows + k * piece_rows, piece_rows), :] = (
            gains * unit * fan_scale
        ).astype(BF16)
        return carry

    pl.semaphore_wait(barrier, 3 + data_count)

    up = copy(cot_hbm.at[pl.ds(0, cols), :], halo.at[1], halo_s.at[0], halo_r.at[1],
              {"space": (band + 3) % 4})
    down = copy(cot_hbm.at[pl.ds(pixels - cols, cols), :], halo.at[0], halo_s.at[1], halo_r.at[0],
                {"space": (band + 1) % 4})

    @pl.when(band > 0)
    def _():
        up.start()

    @pl.when(band < 3)
    def _():
        down.start()

    loads[0].wait()
    loads[1].wait()
    diagonal = lax.broadcasted_iota(jnp.int32, (owner_rows, owner_rows), 0) == (
        lax.broadcasted_iota(jnp.int32, (owner_rows, owner_rows), 1)
    )
    gain_ref[...] = jnp.sum(jnp.where(diagonal, gain_row[...], 0.0), axis=1, keepdims=True)

    lax.fori_loop(0, 4, std_step, 0)

    def std_piece(owner, quarter):
        return std.at[rows_at(owner * owner_rows + quarter * piece_rows, piece_rows), :]

    wz = []
    own = std_piece(mine, slot)
    for t in range(3):
        wz.append(copy(own, own, wz_s.at[t], wz_r.at[mine], {"dp": order[t]}))
        wz[-1].start()

    loads[2].wait()
    loads[3].wait()
    gpad[pl.ds(cols, pixels), :] = (alpha_skip * cot_ref[...].astype(F32)).astype(BF16)

    row_id = lax.broadcasted_iota(jnp.int32, (pixels, width), 0) % cols

    def act_step(g, carry):
        at = pl.ds(pl.multiple_of(g * width, width), width)
        x = x_ref[:, at].astype(F32)
        cdf = 0.5 * (1.0 + lax.erf(x * math.sqrt(0.5)))
        hidden = act_gain * (x * cdf)
        slope[:, at] = act_gain * (cdf + x * (jnp.exp(-0.5 * x * x) * (1.0 / math.sqrt(2.0 * math.pi))))
        before = jnp.where(row_id == 0, 0.0, pltpu.roll(hidden, 1, 0))
        after = jnp.where(row_id == cols - 1, 0.0, pltpu.roll(hidden, pixels - 1, 0))
        for b, value in enumerate((before, hidden, after)):
            hs[:, pl.ds(pl.multiple_of(g * wide + b * width, width), width)] = value.astype(BF16)
        return carry

    lax.fori_loop(0, group_count, act_step, 0)

    @pl.when(band > 0)
    def _():
        down.wait_recv()
        gpad[pl.ds(0, cols), :] = (alpha_skip * halo[0].astype(F32)).astype(BF16)

    @pl.when(band == 0)
    def _():
        gpad[pl.ds(0, cols), :] = jnp.zeros((cols, chan_count), BF16)

    @pl.when(band < 3)
    def _():
        up.wait_recv()
        gpad[pl.ds(cols + pixels, cols), :] = (alpha_skip * halo[1].astype(F32)).astype(BF16)

    @pl.when(band == 3)
    def _():
        gpad[pl.ds(cols + pixels, cols), :] = jnp.zeros((cols, chan_count), BF16)

    def weight_step(g, carry):
        at = pl.ds(pl.multiple_of(g * width, width), width)
        right = hs[:, pl.ds(pl.multiple_of(g * wide, width), wide)]
        for a in range(3):
            left = gpad[pl.ds((2 - a) * cols, pixels), at]
            part[pl.ds(pl.multiple_of(g * width, width), width), pl.ds(a * wide, wide)] = (
                lax.dot_general(left, right, (((0,), (0,)), ((), ())), preferred_element_type=F32)
            )
        return carry

    def place(owner, quarter):
        return rows_at(owner * owner_rows + quarter * piece_rows, piece_rows)

    half_groups = group_count // 2
    rc = []
    for half in range(2):
        first = half_groups * (far_half if half == 0 else 1 - far_half)
        lax.fori_loop(0, half_groups, lambda k, c: weight_step(first + k, c), 0)
        for d in range(2 * half, 2 * half + 2):
            for t in range(2):
                at = place(order[d], 1 - core + 2 * t)
                sendb[at, :] = part[at, :].astype(BF16)
                n = 2 * d + t
                rc.append(copy(sendb.at[at, :], got_core.at[n], rc_s.at[n], rc_r.at[n],
                               {"space": pair}))
                rc[-1].start()

    rx = []
    for d in range(4):
        for t in range(2):
            rc[2 * d + t].wait_recv()
        at = place(order[d], cross)
        sendb[at, :] = (part[at, :] + got_core[2 * d + cross // 2].astype(F32)).astype(BF16)
        rx.append(copy(sendb.at[at, :], got_x.at[d], rx_s.at[d], rx_r.at[d], {"space": cross}))
        rx[-1].start()

    wx = []
    for t in (2, 1, 0):
        piece = std_piece(order[t], slot)
        copy(piece, piece, wz_s.at[t], wz_r.at[order[t]], {"dp": order[t]}).wait_recv()
        wx.append(copy(piece, piece, wx_s.at[t], wx_r.at[t], {"groups": 1 - group}))
        wx[-1].start()

    rz = []
    for d in range(4):
        rx[d].wait_recv()
        at = place(order[d], band)
        total = part[at, :] + got_core[2 * d + band // 2].astype(F32) + got_x[d].astype(F32)
        if d == 3:
            part[at, :] = total
        else:
            sendb[at, :] = total.astype(BF16)
            rz.append(copy(sendb.at[at, :], got_z.at[mine], rz_s.at[d], rz_r.at[mine],
                           {"dp": order[d]}))
            rz[-1].start()

    wc = []
    for n, t in enumerate((2, 1, 0)):
        wx[n].wait_recv()
        for e, quarter in enumerate((slot, slot_cross)):
            piece = std_piece(order[t], quarter)
            wc.append(copy(piece, piece, wc_s.at[2 * t + e], wc_r.at[2 * t + e], {"space": pair}))
            wc[-1].start()
    for one in wc:
        one.wait_recv()

    def back_step(g, carry):
        at = pl.ds(pl.multiple_of(g * width, width), width)
        left = jnp.concatenate(
            [gpad[pl.ds((2 - a) * cols, pixels), at] for a in range(3)], axis=1
        )
        right = jnp.concatenate([std[at, pl.ds(a * wide, wide)] for a in range(3)], axis=0)
        y = jnp.dot(left, right, preferred_element_type=F32)
        low, mid, high = y[:, :width], y[:, width : 2 * width], y[:, 2 * width :]
        low = jnp.where(row_id == cols - 1, 0.0, pltpu.roll(low, pixels - 1, 0))
        high = jnp.where(row_id == 0, 0.0, pltpu.roll(high, 1, 0))
        grad = cot_ref[:, at].astype(F32) + slope[:, at] * (low + mid + high)
        grad_ref[:, at] = grad.astype(BF16)
        return carry

    lax.fori_loop(0, half_groups, back_step, 0)
    outs = []
    half_cols = chan_count // 2

    def write(src, dst):
        outs.append(pltpu.make_async_copy(src, dst, out_s.at[len(outs)]))
        outs[-1].start()

    write(grad_ref.at[:, pl.ds(0, half_cols)], grad_hbm.at[:, pl.ds(0, half_cols)])

    total = part[place(mine, band), :]
    for t in (2, 1, 0):
        here = sendb.at[place(order[t], band), :]
        copy(here, got_z.at[order[t]], rz_s.at[t], rz_r.at[order[t]], {"dp": order[t]}).wait_recv()
        total = total + got_z[order[t]].astype(F32)
    grad_standard = total * (1.0 / total_images)
    rows = rows_at(band * piece_rows, piece_rows)
    gains = gain_ref[rows, :]
    unit, inv_std = unit_of(raw_ref[rows, :])
    grad_gain = jnp.sum(grad_standard * unit, axis=1, keepdims=True) * fan_scale
    grad_unit = grad_standard * gains * fan_scale
    centre_term = jnp.mean(grad_unit, axis=1, keepdims=True)
    along_term = jnp.mean(grad_unit * unit, axis=1, keepdims=True)
    grad_raw = inv_std * (grad_unit - centre_term - unit * along_term)
    high = grad_gain.astype(BF16).astype(F32)
    low = grad_gain - high
    lane = lax.broadcasted_iota(jnp.int32, (piece_rows, 128), 1)
    gathered[band, :, pl.ds(0, fan_size)] = grad_raw.astype(BF16)
    gathered[band, :, pl.ds(fan_size, 128)] = jnp.where(lane == 0, high, low).astype(BF16)
    ag = []
    for n, (quarter, to) in enumerate(((band, cross), (band, pair), (cross, pair))):
        if n == 2:
            lax.fori_loop(half_groups, group_count - 1, back_step, 0)
            ag[0].wait_recv()
        block = gathered.at[quarter]
        ag.append(copy(block, block, ag_s.at[n], ag_r.at[n], {"space": to}))
        ag[-1].start()
    lax.fori_loop(group_count - 1, group_count, back_step, 0)
    write(grad_ref.at[:, pl.ds(half_cols, half_cols)], grad_hbm.at[:, pl.ds(half_cols, half_cols)])
    ag[1].wait_recv()
    ag[2].wait_recv()
    lane_id = lax.broadcasted_iota(jnp.int32, (piece_rows, owner_rows), 1)
    line_id = lax.broadcasted_iota(jnp.int32, (piece_rows, owner_rows), 0)
    gain_line = jnp.zeros((1, owner_rows), F32)
    for q in range(4):
        write(gathered.at[q, :, pl.ds(0, fan_size)], ws_hbm.at[pl.ds(q * piece_rows, piece_rows), :])
        both = gathered[q, :, pl.ds(fan_size, 128)].astype(F32)
        column = both[:, 0:1] + both[:, 1:2]
        gain_line = gain_line + jnp.sum(
            jnp.where(lane_id == line_id + q * piece_rows, column, 0.0), axis=0, keepdims=True
        )
    gains_ref[...] = gain_line

    @pl.when(band > 0)
    def _():
        up.wait_send()

    @pl.when(band < 3)
    def _():
        down.wait_send()

    for one in outs:
        one.wait()
    for one in wz + rc + rx + wx + rz + wc + ag:
        one.wait_send()


def widen_kernel(
    grad_ref, rounded_ref, gains_ref, grad_out, raw_out, gains_out, held, narrow, wide, line, sems
):
    halves = []
    middle = grad_ref.shape[0] // 2
    for k in range(2):
        at = pl.ds(k * middle, middle)
        halves.append((
            pltpu.make_async_copy(grad_ref.at[at, :], held.at[at, :], sems.at[k]),
            pltpu.make_async_copy(held.at[at, :], grad_out.at[at, :], sems.at[2 + k]),
        ))
    rows = narrow.shape[0] // 2
    for k in range(2):
        at = pl.ds(k * rows, rows)
        halves.append((
            pltpu.make_async_copy(rounded_ref.at[at, :], narrow.at[at, :], sems.at[4 + k]),
            pltpu.make_async_copy(wide.at[at, :], raw_out.at[at, :], sems.at[6 + k]),
        ))
    halves.append((
        pltpu.make_async_copy(gains_ref, line, sems.at[8]),
        pltpu.make_async_copy(line, gains_out, sems.at[9]),
    ))
    order = (2, 3, 0, 1, 4)
    for n in order:
        halves[n][0].start()
    for n in order:
        halves[n][0].wait()
        if n in (2, 3):
            at = pl.ds((n - 2) * rows, rows)
            wide[at, :] = narrow[at, :].astype(F32)
        halves[n][1].start()
    for n in order:
        halves[n][1].wait()


def local_kernel(inputs, cotangent, kernel_raw, kernel_gain):
    images, band_rows, band_cols, chan_count = inputs.shape
    owner_rows, fan_size = kernel_raw.shape
    data_count = lax.axis_size("dp")
    pixels = band_rows * band_cols
    piece_rows = owner_rows // 4
    width = fan_size // 9
    dma = pltpu.SemaphoreType.DMA
    peers = data_count - 1
    vmem = pl.BlockSpec(memory_space=pltpu.VMEM)
    hbm = pl.BlockSpec(memory_space=pltpu.HBM)
    grad, rounded, gains = pl.pallas_call(
        functools.partial(block_kernel, images * data_count, data_count),
        out_shape=(
            jax.ShapeDtypeStruct((pixels, chan_count), BF16),
            jax.ShapeDtypeStruct((owner_rows, fan_size), BF16),
            jax.ShapeDtypeStruct((1, owner_rows), F32),
        ),
        in_specs=[hbm] * 4,
        out_specs=(hbm, hbm, vmem),
        scratch_shapes=[
            pltpu.VMEM((pixels, chan_count), BF16),
            pltpu.VMEM((pixels, chan_count), BF16),
            pltpu.VMEM((owner_rows, fan_size), F32),
            pltpu.VMEM((1, owner_rows), F32),
            pltpu.VMEM((owner_rows, 1), F32),
            pltpu.VMEM((pixels, chan_count), BF16),
            dma((4,)), dma((6,)),
            pltpu.VMEM((2, band_cols, chan_count), BF16),
            pltpu.VMEM((pixels + 2 * band_cols, chan_count), BF16),
            pltpu.VMEM((pixels, 3 * chan_count), BF16),
            pltpu.VMEM((pixels, chan_count), F32),
            pltpu.VMEM((chan_count, fan_size), BF16),
            pltpu.VMEM((chan_count, fan_size), F32),
            pltpu.VMEM((chan_count, fan_size), BF16),
            pltpu.VMEM((2 * data_count, piece_rows, fan_size), BF16),
            pltpu.VMEM((data_count, piece_rows, fan_size), BF16),
            pltpu.VMEM((data_count, piece_rows, fan_size), BF16),
            pltpu.VMEM((4, piece_rows, fan_size + 128), BF16),
            dma((2,)), dma((2,)),
            dma((peers,)), dma((data_count,)),
            dma((peers,)), dma((peers,)),
            dma((2 * peers,)), dma((2 * peers,)),
            dma((2 * data_count,)), dma((2 * data_count,)),
            dma((data_count,)), dma((data_count,)),
            dma((peers,)), dma((data_count,)),
            dma((3,)), dma((3,)),
        ],
        compiler_params=pltpu.CompilerParams(
            collective_id=0, has_side_effects=True, vmem_limit_bytes=60 * 1024 * 1024
        ),
        cost_estimate=pl.CostEstimate(
            flops=4 * pixels * chan_count * fan_size,
            bytes_accessed=8 * pixels * chan_count,
            transcendentals=2 * pixels * chan_count,
        ),
    )(
        inputs.reshape(pixels, chan_count),
        cotangent.reshape(pixels, chan_count),
        kernel_raw,
        kernel_gain.reshape(1, owner_rows),
    )
    grad, grad_raw, grad_gain = pl.pallas_call(
        widen_kernel,
        out_shape=(
            jax.ShapeDtypeStruct((pixels, chan_count), BF16),
            jax.ShapeDtypeStruct((owner_rows, fan_size), F32),
            jax.ShapeDtypeStruct((1, owner_rows), F32),
        ),
        in_specs=[hbm] * 3,
        out_specs=(hbm, hbm, hbm),
        scratch_shapes=[
            pltpu.VMEM((pixels, chan_count), BF16),
            pltpu.VMEM((owner_rows, fan_size), BF16),
            pltpu.VMEM((owner_rows, fan_size), F32),
            pltpu.VMEM((1, owner_rows), F32),
            dma((10,)),
        ],
        compiler_params=pltpu.CompilerParams(vmem_limit_bytes=60 * 1024 * 1024),
    )(grad, rounded, gains)
    return (grad.reshape(inputs.shape), grad_raw, grad_gain.reshape(owner_rows))


def solution(mesh):
    placed = (
        P(("groups", "dp"), "space", None, None),
        P(("groups", "dp"), "space", None, None),
        P("dp", None),
        P("dp"),
    )

    def run(inputs, cotangent, kernel_raw, kernel_gain):
        images, rows, cols, chan_count = inputs.shape
        fan_size = kernel_raw.shape[1]
        data_count = mesh.shape["dp"]
        replicas = mesh.shape["groups"] * data_count
        fits = (
            mesh.shape["space"] == 4
            and data_count == 4
            and mesh.shape["groups"] == 2
            and images == replicas
            and chan_count % (64 * data_count) == 0
            and (chan_count // (fan_size // 9)) % 2 == 0
            and fan_size % (9 * 128) == 0
            and cols % 16 == 0
            and rows % 4 == 0
        )
        return jax.shard_map(
            local_kernel if fits else local,
            mesh=mesh,
            in_specs=placed,
            out_specs=(
                P(("groups", "dp"), "space", None, None),
                P(("groups", "dp"), None),
                P(("groups", "dp")),
            ),
            check_vma=False,
        )(inputs, cotangent, kernel_raw, kernel_gain)

    return run
```

```python
import functools
import math

import jax
import jax.numpy as jnp
from jax import lax
from jax.experimental import pallas as pl
from jax.experimental.pallas import tpu as pltpu
from jax.sharding import PartitionSpec as P

act_gain = 1.7015
alpha_skip = 0.2


def padded_2(value, sides, width):
    for axis, dim in sides:
        size, length = (lax.axis_size(axis), value.shape[dim])
        up = [(i, (i + 1) % size) for i in range(size - 1)]
        down = [(j, i) for i, j in up]
        last = lax.slice_in_dim(value, length - width, length, axis=dim)
        first = lax.slice_in_dim(value, 0, width, axis=dim)
        before = lax.ppermute(last, axis, up)
        after = lax.ppermute(first, axis, down)
        value = jnp.concatenate([before, value, after], axis=dim)
    return value


def activate(value_in):
    return act_gain * jax.nn.gelu(value_in, approximate=False)


def ws_parts(kernel_rows):
    row_mean = jnp.mean(kernel_rows, axis=1, keepdims=True)
    centred = kernel_rows - row_mean
    row_var = jnp.mean(centred * centred, axis=1, keepdims=True)
    inv_std = lax.rsqrt(row_var + 1e-05)
    return (centred * inv_std, inv_std)


def ws_back(grad_standard, unit, inv_std, gains):
    fan_scale = 1.0 / math.sqrt(unit.shape[1])
    grad_gain = jnp.sum(grad_standard * unit, axis=1) * fan_scale
    grad_unit = grad_standard * gains[:, None] * fan_scale
    centre_term = jnp.mean(grad_unit, axis=1, keepdims=True)
    along_term = jnp.mean(grad_unit * unit, axis=1, keepdims=True)
    grad_raw = inv_std * (grad_unit - centre_term - unit * along_term)
    return (grad_raw, grad_gain)


def local(inputs, cotangent, kernel_raw, kernel_gain):
    images, band_rows, band_cols, chan_count = inputs.shape
    fan_size = kernel_raw.shape[1]
    group_width = fan_size // 9
    group_count = chan_count // group_width
    fan_scale = 1.0 / math.sqrt(fan_size)
    inputs_wide = inputs.astype(jnp.float32)
    hidden = activate(inputs_wide).astype(jnp.bfloat16)
    grad_conv = (alpha_skip * cotangent.astype(jnp.float32)).astype(jnp.bfloat16)
    stacked = jnp.stack([hidden, grad_conv])
    rimmed = padded_2(stacked, (("space", 2),), 1)
    padded = jnp.pad(rimmed, ((0, 0), (0, 0), (0, 0), (1, 1), (0, 0)))
    hidden_pad = padded[0]
    grad_pad = padded[1]
    unit, inv_std = ws_parts(kernel_raw)
    standard_rows = (kernel_gain[:, None] * unit * fan_scale).astype(jnp.bfloat16)
    standard = lax.all_gather(standard_rows, "dp", axis=0, tiled=True)
    tap_kernels = standard.reshape(group_count, group_width, 3, 3, group_width)
    count = images * band_rows * band_cols
    grad_flat = grad_conv.reshape(count, group_count, group_width)
    grad_hidden = jnp.zeros((count, group_count, group_width), jnp.float32)
    tap_grads = []
    for tap_row in range(3):
        backed_cols = []
        for tap_col in range(3):
            shifted = hidden_pad[:, tap_row : tap_row + band_rows, tap_col : tap_col + band_cols]
            shifted = shifted.reshape(count, group_count, group_width)
            tap_grads.append(
                jnp.einsum("mgo,mgi->goi", grad_flat, shifted, preferred_element_type=jnp.float32)
            )
            backed = grad_pad[
                :, 2 - tap_row : 2 - tap_row + band_rows, 2 - tap_col : 2 - tap_col + band_cols
            ]
            backed_cols.append(backed.reshape(count, group_count, group_width))
        backed_row = jnp.stack(backed_cols, axis=2)
        grad_hidden = grad_hidden + jnp.einsum(
            "mgbo,gobi->mgi",
            backed_row,
            tap_kernels[:, :, tap_row],
            preferred_element_type=jnp.float32,
        )
    total_images = images * lax.axis_size("dp")
    grad_standard = jnp.stack(tap_grads, axis=2).reshape(chan_count, fan_size) * (
        1.0 / total_images
    )
    unused_act, pull_act = jax.vjp(activate, inputs_wide)
    grad_inputs = cotangent.astype(jnp.float32) + pull_act(grad_hidden.reshape(inputs.shape))[0]
    band_count = lax.axis_size("space")
    data_count = lax.axis_size("dp")
    owner_rows = kernel_raw.shape[0]
    piece_rows = owner_rows // band_count
    ordered = grad_standard.reshape(data_count, band_count, piece_rows, fan_size)
    ordered = ordered.transpose(1, 0, 2, 3).reshape(chan_count, fan_size)
    piece = lax.psum_scatter(ordered, ("space", "dp"), scatter_dimension=0, tiled=True)
    start = lax.axis_index("space") * piece_rows
    unit_piece = lax.dynamic_slice_in_dim(unit, start, piece_rows, 0)
    inv_piece = lax.dynamic_slice_in_dim(inv_std, start, piece_rows, 0)
    gain_piece = lax.dynamic_slice_in_dim(kernel_gain, start, piece_rows, 0)
    raw_piece, gain_grad_piece = ws_back(piece, unit_piece, inv_piece, gain_piece)
    grad_raw, grad_gain = (
        lax.all_gather(raw_piece, "space", axis=0, tiled=True),
        lax.all_gather(gain_grad_piece, "space", axis=0, tiled=True),
    )
    return (grad_inputs.astype(jnp.bfloat16), grad_raw, grad_gain)


MESH = pl.DeviceIdType.MESH
F32 = jnp.float32
BF16 = jnp.bfloat16


def rows_at(start, size):
    return pl.ds(pl.multiple_of(start, 16), size)


def block_kernel(
    total_images, data_count,
    x_hbm, cot_hbm, raw_hbm, gain_hbm, grad_hbm, ws_hbm, gains_ref,
    x_ref, cot_ref, raw_ref, gain_row, gain_ref, grad_ref, load_s, out_s, halo, gpad, hs, slope, std, part, sendb, got_core, got_x, got_z, gathered,
    halo_s, halo_r, wz_s, wz_r, wx_s, wx_r, wc_s, wc_r,
    rc_s, rc_r, rx_s, rx_r, rz_s, rz_r, ag_s, ag_r,
):
    pixels, chan_count = x_ref.shape
    owner_rows, fan_size = raw_ref.shape
    width = fan_size // 9
    wide = 3 * width
    group_count = chan_count // width
    cols = gpad.shape[0] - pixels
    cols = cols // 2
    piece_rows = owner_rows // 4
    fan_scale = 1.0 / math.sqrt(fan_size)
    band = lax.axis_index("space")
    mine = lax.axis_index("dp")
    group = lax.axis_index("groups")
    core = band % 2
    slot = 2 * group + core
    slot_cross = 2 * (1 - group) + core
    far_half = 1 - mine // 2
    order = (3 * far_half, 1 + far_half, 2 * (mine // 2) + 1 - mine % 2, mine)
    pair = band + 1 - 2 * core
    cross = (band + 2) % 4

    def copy(src, dst, send, recv, where):
        return pltpu.make_async_remote_copy(
            src_ref=src, dst_ref=dst, send_sem=send, recv_sem=recv,
            device_id=where, device_id_type=MESH,
        )

    barrier = pltpu.get_barrier_semaphore()
    for j in range(1, 4):
        pl.semaphore_signal(
            barrier, inc=1, device_id={"space": (band + j) % 4}, device_id_type=MESH
        )
    for j in range(1, data_count):
        pl.semaphore_signal(
            barrier, inc=1, device_id={"dp": (mine + j) % data_count}, device_id_type=MESH
        )

    pl.semaphore_signal(barrier, inc=1, device_id={"groups": 1 - group}, device_id_type=MESH)

    loads = [
        pltpu.make_async_copy(src, dst, load_s.at[n])
        for n, (src, dst) in enumerate(
            ((raw_hbm, raw_ref), (gain_hbm, gain_row), (x_hbm, x_ref), (cot_hbm, cot_ref))
        )
    ]
    for one in loads:
        one.start()

    def unit_of(rows):
        row_mean = jnp.mean(rows, axis=1, keepdims=True)
        centred = rows - row_mean
        row_var = jnp.mean(centred * centred, axis=1, keepdims=True)
        inv_std = lax.rsqrt(row_var + 1e-05)
        return centred * inv_std, inv_std

    def std_step(k, carry):
        rows = rows_at(k * piece_rows, piece_rows)
        gains = gain_ref[rows, :]
        unit, _ = unit_of(raw_ref[rows, :])
        std[rows_at(mine * owner_rows + k * piece_rows, piece_rows), :] = (
            gains * unit * fan_scale
        ).astype(BF16)
        return carry

    pl.semaphore_wait(barrier, 3 + data_count)

    up = copy(cot_hbm.at[pl.ds(0, cols), :], halo.at[1], halo_s.at[0], halo_r.at[1],
              {"space": (band + 3) % 4})
    down = copy(cot_hbm.at[pl.ds(pixels - cols, cols), :], halo.at[0], halo_s.at[1], halo_r.at[0],
                {"space": (band + 1) % 4})

    @pl.when(band > 0)
    def _():
        up.start()

    @pl.when(band < 3)
    def _():
        down.start()

    loads[0].wait()
    loads[1].wait()
    diagonal = lax.broadcasted_iota(jnp.int32, (owner_rows, owner_rows), 0) == (
        lax.broadcasted_iota(jnp.int32, (owner_rows, owner_rows), 1)
    )
    gain_ref[...] = jnp.sum(jnp.where(diagonal, gain_row[...], 0.0), axis=1, keepdims=True)

    lax.fori_loop(0, 4, std_step, 0)

    def std_piece(owner, quarter):
        return std.at[rows_at(owner * owner_rows + quarter * piece_rows, piece_rows), :]

    wz = []
    own = std_piece(mine, slot)
    for t in (2, 1, 0):
        wz.append(copy(own, own, wz_s.at[t], wz_r.at[mine], {"dp": order[t]}))
        wz[-1].start()

    loads[2].wait()
    loads[3].wait()
    gpad[pl.ds(cols, pixels), :] = (alpha_skip * cot_ref[...].astype(F32)).astype(BF16)

    row_id = lax.broadcasted_iota(jnp.int32, (pixels, width), 0) % cols

    def act_step(g, carry):
        at = pl.ds(pl.multiple_of(g * width, width), width)
        x = x_ref[:, at].astype(F32)
        cdf = 0.5 * (1.0 + lax.erf(x * math.sqrt(0.5)))
        hidden = act_gain * (x * cdf)
        slope[:, at] = act_gain * (cdf + x * (jnp.exp(-0.5 * x * x) * (1.0 / math.sqrt(2.0 * math.pi))))
        before = jnp.where(row_id == 0, 0.0, pltpu.roll(hidden, 1, 0))
        after = jnp.where(row_id == cols - 1, 0.0, pltpu.roll(hidden, pixels - 1, 0))
        for b, value in enumerate((before, hidden, after)):
            hs[:, pl.ds(pl.multiple_of(g * wide + b * width, width), width)] = value.astype(BF16)
        return carry

    lax.fori_loop(0, group_count, act_step, 0)

    def taps(g, chosen):
        at = pl.ds(pl.multiple_of(g * width, width), width)
        right = hs[:, pl.ds(pl.multiple_of(g * wide, width), wide)]
        for a in chosen:
            left = gpad[pl.ds((2 - a) * cols, pixels), at]
            part[at, pl.ds(a * wide, wide)] = lax.dot_general(
                left, right, (((0,), (0,)), ((), ())), preferred_element_type=F32
            )

    def middle_step(g, carry):
        taps(g, (1,))
        return carry

    lax.fori_loop(0, group_count, middle_step, 0)

    @pl.when(band > 0)
    def _():
        down.wait_recv()
        gpad[pl.ds(0, cols), :] = (alpha_skip * halo[0].astype(F32)).astype(BF16)

    @pl.when(band == 0)
    def _():
        gpad[pl.ds(0, cols), :] = jnp.zeros((cols, chan_count), BF16)

    @pl.when(band < 3)
    def _():
        up.wait_recv()
        gpad[pl.ds(cols + pixels, cols), :] = (alpha_skip * halo[1].astype(F32)).astype(BF16)

    @pl.when(band == 3)
    def _():
        gpad[pl.ds(cols + pixels, cols), :] = jnp.zeros((cols, chan_count), BF16)

    def weight_step(g, carry):
        taps(g, (0, 2))
        return carry

    def place(owner, quarter):
        return rows_at(owner * owner_rows + quarter * piece_rows, piece_rows)

    half_groups = group_count // 2
    wx = []

    def forward(t):
        piece = std_piece(order[t], slot)
        copy(piece, piece, wz_s.at[t], wz_r.at[order[t]], {"dp": order[t]}).wait_recv()
        wx.append(copy(piece, piece, wx_s.at[t], wx_r.at[t], {"groups": 1 - group}))
        wx[-1].start()

    rc = []
    for half in range(2):
        first = half_groups * (far_half if half == 0 else 1 - far_half)
        lax.fori_loop(0, half_groups, lambda k, c: weight_step(first + k, c), 0)
        for d in range(2 * half, 2 * half + 2):
            for t in range(2):
                at = place(order[d], 1 - core + 2 * t)
                sendb[at, :] = part[at, :].astype(BF16)
                n = 2 * d + t
                rc.append(copy(sendb.at[at, :], got_core.at[n], rc_s.at[n], rc_r.at[n],
                               {"space": pair}))
                rc[-1].start()

    rx = []
    for d in range(4):
        for t in range(2):
            rc[2 * d + t].wait_recv()
        at = place(order[d], cross)
        sendb[at, :] = (part[at, :] + got_core[2 * d + cross // 2].astype(F32)).astype(BF16)
        rx.append(copy(sendb.at[at, :], got_x.at[d], rx_s.at[d], rx_r.at[d], {"space": cross}))
        rx[-1].start()
        if d > 0:
            forward(3 - d)

    wc = []

    def forward_pair(n):
        t = 2 - n
        wx[n].wait_recv()
        for e, quarter in enumerate((slot, slot_cross)):
            piece = std_piece(order[t], quarter)
            wc.append(copy(piece, piece, wc_s.at[2 * t + e], wc_r.at[2 * t + e], {"space": pair}))
            wc[-1].start()

    rz = []
    for d in range(4):
        rx[d].wait_recv()
        at = place(order[d], band)
        total = part[at, :] + got_core[2 * d + band // 2].astype(F32) + got_x[d].astype(F32)
        if d == 3:
            part[at, :] = total
        else:
            sendb[at, :] = total.astype(BF16)
            rz.append(copy(sendb.at[at, :], got_z.at[mine], rz_s.at[d], rz_r.at[mine],
                           {"dp": order[d]}))
            rz[-1].start()
        if d > 0:
            forward_pair(d - 1)

    for one in wc:
        one.wait_recv()

    def back_step(g, carry):
        at = pl.ds(pl.multiple_of(g * width, width), width)
        left = jnp.concatenate(
            [gpad[pl.ds((2 - a) * cols, pixels), at] for a in range(3)], axis=1
        )
        right = jnp.concatenate([std[at, pl.ds(a * wide, wide)] for a in range(3)], axis=0)
        y = jnp.dot(left, right, preferred_element_type=F32)
        low, mid, high = y[:, :width], y[:, width : 2 * width], y[:, 2 * width :]
        low = jnp.where(row_id == cols - 1, 0.0, pltpu.roll(low, pixels - 1, 0))
        high = jnp.where(row_id == 0, 0.0, pltpu.roll(high, 1, 0))
        grad = cot_ref[:, at].astype(F32) + slope[:, at] * (low + mid + high)
        grad_ref[:, at] = grad.astype(BF16)
        return carry

    lax.fori_loop(0, half_groups, back_step, 0)
    outs = []
    half_cols = chan_count // 2

    def write(src, dst):
        outs.append(pltpu.make_async_copy(src, dst, out_s.at[len(outs)]))
        outs[-1].start()

    write(grad_ref.at[:, pl.ds(0, half_cols)], grad_hbm.at[:, pl.ds(0, half_cols)])

    total = part[place(mine, band), :]
    for t in (2, 1, 0):
        here = sendb.at[place(order[t], band), :]
        copy(here, got_z.at[order[t]], rz_s.at[t], rz_r.at[order[t]], {"dp": order[t]}).wait_recv()
        total = total + got_z[order[t]].astype(F32)
    grad_standard = total * (1.0 / total_images)
    rows = rows_at(band * piece_rows, piece_rows)
    gains = gain_ref[rows, :]
    unit, inv_std = unit_of(raw_ref[rows, :])
    grad_gain = jnp.sum(grad_standard * unit, axis=1, keepdims=True) * fan_scale
    grad_unit = grad_standard * gains * fan_scale
    centre_term = jnp.mean(grad_unit, axis=1, keepdims=True)
    along_term = jnp.mean(grad_unit * unit, axis=1, keepdims=True)
    grad_raw = inv_std * (grad_unit - centre_term - unit * along_term)
    high = grad_gain.astype(BF16).astype(F32)
    low = grad_gain - high
    lane = lax.broadcasted_iota(jnp.int32, (piece_rows, 128), 1)
    gathered[band, :, pl.ds(0, fan_size)] = grad_raw.astype(BF16)
    gathered[band, :, pl.ds(fan_size, 128)] = jnp.where(lane == 0, high, low).astype(BF16)
    ag = []
    for n, (quarter, to) in enumerate(((band, cross), (band, pair), (cross, pair))):
        if n == 2:
            lax.fori_loop(half_groups, group_count - 1, back_step, 0)
            ag[0].wait_recv()
        block = gathered.at[quarter]
        ag.append(copy(block, block, ag_s.at[n], ag_r.at[n], {"space": to}))
        ag[-1].start()
    lax.fori_loop(group_count - 1, group_count, back_step, 0)
    write(grad_ref.at[:, pl.ds(half_cols, half_cols)], grad_hbm.at[:, pl.ds(half_cols, half_cols)])
    ag[1].wait_recv()
    ag[2].wait_recv()
    lane_id = lax.broadcasted_iota(jnp.int32, (piece_rows, owner_rows), 1)
    line_id = lax.broadcasted_iota(jnp.int32, (piece_rows, owner_rows), 0)
    gain_line = jnp.zeros((1, owner_rows), F32)
    for q in range(4):
        write(gathered.at[q, :, pl.ds(0, fan_size)], ws_hbm.at[pl.ds(q * piece_rows, piece_rows), :])
        both = gathered[q, :, pl.ds(fan_size, 128)].astype(F32)
        column = both[:, 0:1] + both[:, 1:2]
        gain_line = gain_line + jnp.sum(
            jnp.where(lane_id == line_id + q * piece_rows, column, 0.0), axis=0, keepdims=True
        )
    gains_ref[...] = gain_line

    @pl.when(band > 0)
    def _():
        up.wait_send()

    @pl.when(band < 3)
    def _():
        down.wait_send()

    for one in outs:
        one.wait()
    for one in wz + rc + rx + wx + rz + wc + ag:
        one.wait_send()


def widen_kernel(
    grad_ref, rounded_ref, gains_ref, grad_out, raw_out, gains_out, held, narrow, wide, line, sems
):
    halves = []
    middle = grad_ref.shape[0] // 2
    for k in range(2):
        at = pl.ds(k * middle, middle)
        halves.append((
            pltpu.make_async_copy(grad_ref.at[at, :], held.at[at, :], sems.at[k]),
            pltpu.make_async_copy(held.at[at, :], grad_out.at[at, :], sems.at[2 + k]),
        ))
    rows = narrow.shape[0] // 2
    for k in range(2):
        at = pl.ds(k * rows, rows)
        halves.append((
            pltpu.make_async_copy(rounded_ref.at[at, :], narrow.at[at, :], sems.at[4 + k]),
            pltpu.make_async_copy(wide.at[at, :], raw_out.at[at, :], sems.at[6 + k]),
        ))
    halves.append((
        pltpu.make_async_copy(gains_ref, line, sems.at[8]),
        pltpu.make_async_copy(line, gains_out, sems.at[9]),
    ))
    order = (2, 3, 0, 1, 4)
    for n in order:
        halves[n][0].start()
    for n in order:
        halves[n][0].wait()
        if n in (2, 3):
            at = pl.ds((n - 2) * rows, rows)
            wide[at, :] = narrow[at, :].astype(F32)
        halves[n][1].start()
    for n in order:
        halves[n][1].wait()


def local_kernel(inputs, cotangent, kernel_raw, kernel_gain):
    images, band_rows, band_cols, chan_count = inputs.shape
    owner_rows, fan_size = kernel_raw.shape
    data_count = lax.axis_size("dp")
    pixels = band_rows * band_cols
    piece_rows = owner_rows // 4
    width = fan_size // 9
    dma = pltpu.SemaphoreType.DMA
    peers = data_count - 1
    vmem = pl.BlockSpec(memory_space=pltpu.VMEM)
    hbm = pl.BlockSpec(memory_space=pltpu.HBM)
    grad, rounded, gains = pl.pallas_call(
        functools.partial(block_kernel, images * data_count, data_count),
        out_shape=(
            jax.ShapeDtypeStruct((pixels, chan_count), BF16),
            jax.ShapeDtypeStruct((owner_rows, fan_size), BF16),
            jax.ShapeDtypeStruct((1, owner_rows), F32),
        ),
        in_specs=[hbm] * 4,
        out_specs=(hbm, hbm, vmem),
        scratch_shapes=[
            pltpu.VMEM((pixels, chan_count), BF16),
            pltpu.VMEM((pixels, chan_count), BF16),
            pltpu.VMEM((owner_rows, fan_size), F32),
            pltpu.VMEM((1, owner_rows), F32),
            pltpu.VMEM((owner_rows, 1), F32),
            pltpu.VMEM((pixels, chan_count), BF16),
            dma((4,)), dma((6,)),
            pltpu.VMEM((2, band_cols, chan_count), BF16),
            pltpu.VMEM((pixels + 2 * band_cols, chan_count), BF16),
            pltpu.VMEM((pixels, 3 * chan_count), BF16),
            pltpu.VMEM((pixels, chan_count), F32),
            pltpu.VMEM((chan_count, fan_size), BF16),
            pltpu.VMEM((chan_count, fan_size), F32),
            pltpu.VMEM((chan_count, fan_size), BF16),
            pltpu.VMEM((2 * data_count, piece_rows, fan_size), BF16),
            pltpu.VMEM((data_count, piece_rows, fan_size), BF16),
            pltpu.VMEM((data_count, piece_rows, fan_size), BF16),
            pltpu.VMEM((4, piece_rows, fan_size + 128), BF16),
            dma((2,)), dma((2,)),
            dma((peers,)), dma((data_count,)),
            dma((peers,)), dma((peers,)),
            dma((2 * peers,)), dma((2 * peers,)),
            dma((2 * data_count,)), dma((2 * data_count,)),
            dma((data_count,)), dma((data_count,)),
            dma((peers,)), dma((data_count,)),
            dma((3,)), dma((3,)),
        ],
        compiler_params=pltpu.CompilerParams(
            collective_id=0, has_side_effects=True, vmem_limit_bytes=60 * 1024 * 1024
        ),
        cost_estimate=pl.CostEstimate(
            flops=4 * pixels * chan_count * fan_size,
            bytes_accessed=8 * pixels * chan_count,
            transcendentals=2 * pixels * chan_count,
        ),
    )(
        inputs.reshape(pixels, chan_count),
        cotangent.reshape(pixels, chan_count),
        kernel_raw,
        kernel_gain.reshape(1, owner_rows),
    )
    grad, grad_raw, grad_gain = pl.pallas_call(
        widen_kernel,
        out_shape=(
            jax.ShapeDtypeStruct((pixels, chan_count), BF16),
            jax.ShapeDtypeStruct((owner_rows, fan_size), F32),
            jax.ShapeDtypeStruct((1, owner_rows), F32),
        ),
        in_specs=[hbm] * 3,
        out_specs=(hbm, hbm, hbm),
        scratch_shapes=[
            pltpu.VMEM((pixels, chan_count), BF16),
            pltpu.VMEM((owner_rows, fan_size), BF16),
            pltpu.VMEM((owner_rows, fan_size), F32),
            pltpu.VMEM((1, owner_rows), F32),
            dma((10,)),
        ],
        compiler_params=pltpu.CompilerParams(vmem_limit_bytes=60 * 1024 * 1024),
    )(grad, rounded, gains)
    return (grad.reshape(inputs.shape), grad_raw, grad_gain.reshape(owner_rows))


def solution(mesh):
    placed = (
        P(("groups", "dp"), "space", None, None),
        P(("groups", "dp"), "space", None, None),
        P("dp", None),
        P("dp"),
    )

    def run(inputs, cotangent, kernel_raw, kernel_gain):
        images, rows, cols, chan_count = inputs.shape
        fan_size = kernel_raw.shape[1]
        data_count = mesh.shape["dp"]
        replicas = mesh.shape["groups"] * data_count
        fits = (
            mesh.shape["space"] == 4
            and data_count == 4
            and mesh.shape["groups"] == 2
            and images == replicas
            and chan_count % (64 * data_count) == 0
            and (chan_count // (fan_size // 9)) % 2 == 0
            and fan_size % (9 * 128) == 0
            and cols % 16 == 0
            and rows % 4 == 0
        )
        return jax.shard_map(
            local_kernel if fits else local,
            mesh=mesh,
            in_specs=placed,
            out_specs=(
                P(("groups", "dp"), "space", None, None),
                P(("groups", "dp"), None),
                P(("groups", "dp")),
            ),
            check_vma=False,
        )(inputs, cotangent, kernel_raw, kernel_gain)

    return run
```

```python
import functools
import math

import jax
import jax.numpy as jnp
from jax import lax
from jax.experimental import pallas as pl
from jax.experimental.pallas import tpu as pltpu
from jax.sharding import PartitionSpec as P

act_gain = 1.7015
alpha_skip = 0.2


def padded_2(value, sides, width):
    for axis, dim in sides:
        size, length = (lax.axis_size(axis), value.shape[dim])
        up = [(i, (i + 1) % size) for i in range(size - 1)]
        down = [(j, i) for i, j in up]
        last = lax.slice_in_dim(value, length - width, length, axis=dim)
        first = lax.slice_in_dim(value, 0, width, axis=dim)
        before = lax.ppermute(last, axis, up)
        after = lax.ppermute(first, axis, down)
        value = jnp.concatenate([before, value, after], axis=dim)
    return value


def activate(value_in):
    return act_gain * jax.nn.gelu(value_in, approximate=False)


def ws_parts(kernel_rows):
    row_mean = jnp.mean(kernel_rows, axis=1, keepdims=True)
    centred = kernel_rows - row_mean
    row_var = jnp.mean(centred * centred, axis=1, keepdims=True)
    inv_std = lax.rsqrt(row_var + 1e-05)
    return (centred * inv_std, inv_std)


def ws_back(grad_standard, unit, inv_std, gains):
    fan_scale = 1.0 / math.sqrt(unit.shape[1])
    grad_gain = jnp.sum(grad_standard * unit, axis=1) * fan_scale
    grad_unit = grad_standard * gains[:, None] * fan_scale
    centre_term = jnp.mean(grad_unit, axis=1, keepdims=True)
    along_term = jnp.mean(grad_unit * unit, axis=1, keepdims=True)
    grad_raw = inv_std * (grad_unit - centre_term - unit * along_term)
    return (grad_raw, grad_gain)


def local(inputs, cotangent, kernel_raw, kernel_gain):
    images, band_rows, band_cols, chan_count = inputs.shape
    fan_size = kernel_raw.shape[1]
    group_width = fan_size // 9
    group_count = chan_count // group_width
    fan_scale = 1.0 / math.sqrt(fan_size)
    inputs_wide = inputs.astype(jnp.float32)
    hidden = activate(inputs_wide).astype(jnp.bfloat16)
    grad_conv = (alpha_skip * cotangent.astype(jnp.float32)).astype(jnp.bfloat16)
    stacked = jnp.stack([hidden, grad_conv])
    rimmed = padded_2(stacked, (("space", 2),), 1)
    padded = jnp.pad(rimmed, ((0, 0), (0, 0), (0, 0), (1, 1), (0, 0)))
    hidden_pad = padded[0]
    grad_pad = padded[1]
    unit, inv_std = ws_parts(kernel_raw)
    standard_rows = (kernel_gain[:, None] * unit * fan_scale).astype(jnp.bfloat16)
    standard = lax.all_gather(standard_rows, "dp", axis=0, tiled=True)
    tap_kernels = standard.reshape(group_count, group_width, 3, 3, group_width)
    count = images * band_rows * band_cols
    grad_flat = grad_conv.reshape(count, group_count, group_width)
    grad_hidden = jnp.zeros((count, group_count, group_width), jnp.float32)
    tap_grads = []
    for tap_row in range(3):
        backed_cols = []
        for tap_col in range(3):
            shifted = hidden_pad[:, tap_row : tap_row + band_rows, tap_col : tap_col + band_cols]
            shifted = shifted.reshape(count, group_count, group_width)
            tap_grads.append(
                jnp.einsum("mgo,mgi->goi", grad_flat, shifted, preferred_element_type=jnp.float32)
            )
            backed = grad_pad[
                :, 2 - tap_row : 2 - tap_row + band_rows, 2 - tap_col : 2 - tap_col + band_cols
            ]
            backed_cols.append(backed.reshape(count, group_count, group_width))
        backed_row = jnp.stack(backed_cols, axis=2)
        grad_hidden = grad_hidden + jnp.einsum(
            "mgbo,gobi->mgi",
            backed_row,
            tap_kernels[:, :, tap_row],
            preferred_element_type=jnp.float32,
        )
    total_images = images * lax.axis_size("dp")
    grad_standard = jnp.stack(tap_grads, axis=2).reshape(chan_count, fan_size) * (
        1.0 / total_images
    )
    unused_act, pull_act = jax.vjp(activate, inputs_wide)
    grad_inputs = cotangent.astype(jnp.float32) + pull_act(grad_hidden.reshape(inputs.shape))[0]
    band_count = lax.axis_size("space")
    data_count = lax.axis_size("dp")
    owner_rows = kernel_raw.shape[0]
    piece_rows = owner_rows // band_count
    ordered = grad_standard.reshape(data_count, band_count, piece_rows, fan_size)
    ordered = ordered.transpose(1, 0, 2, 3).reshape(chan_count, fan_size)
    piece = lax.psum_scatter(ordered, ("space", "dp"), scatter_dimension=0, tiled=True)
    start = lax.axis_index("space") * piece_rows
    unit_piece = lax.dynamic_slice_in_dim(unit, start, piece_rows, 0)
    inv_piece = lax.dynamic_slice_in_dim(inv_std, start, piece_rows, 0)
    gain_piece = lax.dynamic_slice_in_dim(kernel_gain, start, piece_rows, 0)
    raw_piece, gain_grad_piece = ws_back(piece, unit_piece, inv_piece, gain_piece)
    grad_raw, grad_gain = (
        lax.all_gather(raw_piece, "space", axis=0, tiled=True),
        lax.all_gather(gain_grad_piece, "space", axis=0, tiled=True),
    )
    return (grad_inputs.astype(jnp.bfloat16), grad_raw, grad_gain)


MESH = pl.DeviceIdType.MESH
F32 = jnp.float32
BF16 = jnp.bfloat16


def rows_at(start, size):
    return pl.ds(pl.multiple_of(start, 16), size)


def block_kernel(
    total_images, data_count,
    x_hbm, cot_hbm, raw_hbm, gain_hbm, grad_hbm, ws_hbm, gains_ref,
    x_ref, cot_ref, raw_ref, gain_row, gain_ref, grad_ref, load_s, out_s, halo, gpad, hs, slope, std, part, sendb, got_core, got_x, got_z, gathered,
    halo_s, halo_r, wz_s, wz_r, wx_s, wx_r, wc_s, wc_r,
    rc_s, rc_r, rx_s, rx_r, rz_s, rz_r, ag_s, ag_r,
):
    pixels, chan_count = x_ref.shape
    owner_rows, fan_size = raw_ref.shape
    width = fan_size // 9
    wide = 3 * width
    group_count = chan_count // width
    cols = gpad.shape[0] - pixels
    cols = cols // 2
    piece_rows = owner_rows // 4
    fan_scale = 1.0 / math.sqrt(fan_size)
    band = lax.axis_index("space")
    mine = lax.axis_index("dp")
    group = lax.axis_index("groups")
    core = band % 2
    slot = 2 * group + core
    slot_cross = 2 * (1 - group) + core
    far_half = 1 - mine // 2
    order = (3 * far_half, 1 + far_half, 2 * (mine // 2) + 1 - mine % 2, mine)
    pair = band + 1 - 2 * core
    cross = (band + 2) % 4

    def copy(src, dst, send, recv, where):
        return pltpu.make_async_remote_copy(
            src_ref=src, dst_ref=dst, send_sem=send, recv_sem=recv,
            device_id=where, device_id_type=MESH,
        )

    barrier = pltpu.get_barrier_semaphore()
    for j in range(1, 4):
        pl.semaphore_signal(
            barrier, inc=1, device_id={"space": (band + j) % 4}, device_id_type=MESH
        )
    for j in range(1, data_count):
        pl.semaphore_signal(
            barrier, inc=1, device_id={"dp": (mine + j) % data_count}, device_id_type=MESH
        )

    pl.semaphore_signal(barrier, inc=1, device_id={"groups": 1 - group}, device_id_type=MESH)

    loads = [
        pltpu.make_async_copy(src, dst, load_s.at[n])
        for n, (src, dst) in enumerate(
            ((raw_hbm, raw_ref), (gain_hbm, gain_row), (x_hbm, x_ref), (cot_hbm, cot_ref))
        )
    ]
    for one in loads:
        one.start()

    def unit_of(rows):
        row_mean = jnp.mean(rows, axis=1, keepdims=True)
        centred = rows - row_mean
        row_var = jnp.mean(centred * centred, axis=1, keepdims=True)
        inv_std = lax.rsqrt(row_var + 1e-05)
        return centred * inv_std, inv_std

    def std_step(k, carry):
        rows = rows_at(k * piece_rows, piece_rows)
        gains = gain_ref[rows, :]
        unit, _ = unit_of(raw_ref[rows, :])
        std[rows_at(mine * owner_rows + k * piece_rows, piece_rows), :] = (
            gains * unit * fan_scale
        ).astype(BF16)
        return carry

    pl.semaphore_wait(barrier, 3 + data_count)

    up = copy(cot_hbm.at[pl.ds(0, cols), :], halo.at[1], halo_s.at[0], halo_r.at[1],
              {"space": (band + 3) % 4})
    down = copy(cot_hbm.at[pl.ds(pixels - cols, cols), :], halo.at[0], halo_s.at[1], halo_r.at[0],
                {"space": (band + 1) % 4})

    @pl.when(band > 0)
    def _():
        up.start()

    @pl.when(band < 3)
    def _():
        down.start()

    loads[0].wait()
    loads[1].wait()
    diagonal = lax.broadcasted_iota(jnp.int32, (owner_rows, owner_rows), 0) == (
        lax.broadcasted_iota(jnp.int32, (owner_rows, owner_rows), 1)
    )
    gain_ref[...] = jnp.sum(jnp.where(diagonal, gain_row[...], 0.0), axis=1, keepdims=True)

    lax.fori_loop(0, 4, std_step, 0)

    def std_piece(owner, quarter):
        return std.at[rows_at(owner * owner_rows + quarter * piece_rows, piece_rows), :]

    wz = []
    own = std_piece(mine, slot)
    for t in (2, 1, 0):
        wz.append(copy(own, own, wz_s.at[t], wz_r.at[mine], {"dp": order[t]}))
        wz[-1].start()

    loads[2].wait()
    loads[3].wait()
    gpad[pl.ds(cols, pixels), :] = (alpha_skip * cot_ref[...].astype(F32)).astype(BF16)

    row_id = lax.broadcasted_iota(jnp.int32, (pixels, width), 0) % cols

    def act_step(g, carry):
        at = pl.ds(pl.multiple_of(g * width, width), width)
        x = x_ref[:, at].astype(F32)
        cdf = 0.5 * (1.0 + lax.erf(x * math.sqrt(0.5)))
        hidden = act_gain * (x * cdf)
        slope[:, at] = act_gain * (cdf + x * (jnp.exp(-0.5 * x * x) * (1.0 / math.sqrt(2.0 * math.pi))))
        before = jnp.where(row_id == 0, 0.0, pltpu.roll(hidden, 1, 0))
        after = jnp.where(row_id == cols - 1, 0.0, pltpu.roll(hidden, pixels - 1, 0))
        for b, value in enumerate((before, hidden, after)):
            hs[:, pl.ds(pl.multiple_of(g * wide + b * width, width), width)] = value.astype(BF16)
        return carry

    lax.fori_loop(0, group_count, act_step, 0)

    def taps(g, chosen):
        at = pl.ds(pl.multiple_of(g * width, width), width)
        right = hs[:, pl.ds(pl.multiple_of(g * wide, width), wide)]
        for a in chosen:
            left = gpad[pl.ds((2 - a) * cols, pixels), at]
            part[at, pl.ds(a * wide, wide)] = lax.dot_general(
                left, right, (((0,), (0,)), ((), ())), preferred_element_type=F32
            )

    def middle_step(g, carry):
        taps(g, (1,))
        return carry

    lax.fori_loop(0, group_count, middle_step, 0)

    @pl.when(band > 0)
    def _():
        down.wait_recv()
        gpad[pl.ds(0, cols), :] = (alpha_skip * halo[0].astype(F32)).astype(BF16)

    @pl.when(band == 0)
    def _():
        gpad[pl.ds(0, cols), :] = jnp.zeros((cols, chan_count), BF16)

    @pl.when(band < 3)
    def _():
        up.wait_recv()
        gpad[pl.ds(cols + pixels, cols), :] = (alpha_skip * halo[1].astype(F32)).astype(BF16)

    @pl.when(band == 3)
    def _():
        gpad[pl.ds(cols + pixels, cols), :] = jnp.zeros((cols, chan_count), BF16)

    def weight_step(g, carry):
        taps(g, (0, 2))
        return carry

    def place(owner, quarter):
        return rows_at(owner * owner_rows + quarter * piece_rows, piece_rows)

    half_groups = group_count // 2
    wx = []

    def forward(t):
        piece = std_piece(order[t], slot)
        copy(piece, piece, wz_s.at[t], wz_r.at[order[t]], {"dp": order[t]}).wait_recv()
        wx.append(copy(piece, piece, wx_s.at[t], wx_r.at[t], {"groups": 1 - group}))
        wx[-1].start()

    rc = {}
    for half in range(2):
        first = half_groups * (far_half if half == 0 else 1 - far_half)
        lax.fori_loop(0, half_groups, lambda k, c: weight_step(first + k, c), 0)
        for t, line in enumerate((cross // 2, band // 2)):
            for d in range(2 * half, 2 * half + 2):
                at = place(order[d], 1 - core + 2 * line)
                sendb[at, :] = part[at, :].astype(BF16)
                n = 2 * d + t
                rc[n] = copy(sendb.at[at, :], got_core.at[n], rc_s.at[n], rc_r.at[n],
                             {"space": pair})
                rc[n].start()

    rx = []
    for d in range(4):
        rc[2 * d].wait_recv()
        at = place(order[d], cross)
        sendb[at, :] = (part[at, :] + got_core[2 * d].astype(F32)).astype(BF16)
        rx.append(copy(sendb.at[at, :], got_x.at[d], rx_s.at[d], rx_r.at[d], {"space": cross}))
        rx[-1].start()
        if d > 0:
            forward(3 - d)

    wc = []

    def forward_pair(n):
        t = 2 - n
        wx[n].wait_recv()
        for e, quarter in enumerate((slot, slot_cross)):
            piece = std_piece(order[t], quarter)
            wc.append(copy(piece, piece, wc_s.at[2 * t + e], wc_r.at[2 * t + e], {"space": pair}))
            wc[-1].start()

    rz = []
    for d in range(4):
        rc[2 * d + 1].wait_recv()
        rx[d].wait_recv()
        at = place(order[d], band)
        total = part[at, :] + got_core[2 * d + 1].astype(F32) + got_x[d].astype(F32)
        if d == 3:
            part[at, :] = total
        else:
            sendb[at, :] = total.astype(BF16)
            rz.append(copy(sendb.at[at, :], got_z.at[mine], rz_s.at[d], rz_r.at[mine],
                           {"dp": order[d]}))
            rz[-1].start()
        if d > 0:
            forward_pair(d - 1)

    for one in wc:
        one.wait_recv()

    def back_step(g, carry):
        at = pl.ds(pl.multiple_of(g * width, width), width)
        left = jnp.concatenate(
            [gpad[pl.ds((2 - a) * cols, pixels), at] for a in range(3)], axis=1
        )
        right = jnp.concatenate([std[at, pl.ds(a * wide, wide)] for a in range(3)], axis=0)
        y = jnp.dot(left, right, preferred_element_type=F32)
        low, mid, high = y[:, :width], y[:, width : 2 * width], y[:, 2 * width :]
        low = jnp.where(row_id == cols - 1, 0.0, pltpu.roll(low, pixels - 1, 0))
        high = jnp.where(row_id == 0, 0.0, pltpu.roll(high, 1, 0))
        grad = cot_ref[:, at].astype(F32) + slope[:, at] * (low + mid + high)
        grad_ref[:, at] = grad.astype(BF16)
        return carry

    lax.fori_loop(0, half_groups, back_step, 0)
    outs = []
    half_cols = chan_count // 2

    def write(src, dst):
        outs.append(pltpu.make_async_copy(src, dst, out_s.at[len(outs)]))
        outs[-1].start()

    write(grad_ref.at[:, pl.ds(0, half_cols)], grad_hbm.at[:, pl.ds(0, half_cols)])

    total = part[place(mine, band), :]
    for t in (2, 1, 0):
        here = sendb.at[place(order[t], band), :]
        copy(here, got_z.at[order[t]], rz_s.at[t], rz_r.at[order[t]], {"dp": order[t]}).wait_recv()
        total = total + got_z[order[t]].astype(F32)
    grad_standard = total * (1.0 / total_images)
    rows = rows_at(band * piece_rows, piece_rows)
    gains = gain_ref[rows, :]
    unit, inv_std = unit_of(raw_ref[rows, :])
    grad_gain = jnp.sum(grad_standard * unit, axis=1, keepdims=True) * fan_scale
    grad_unit = grad_standard * gains * fan_scale
    centre_term = jnp.mean(grad_unit, axis=1, keepdims=True)
    along_term = jnp.mean(grad_unit * unit, axis=1, keepdims=True)
    grad_raw = inv_std * (grad_unit - centre_term - unit * along_term)
    high = grad_gain.astype(BF16).astype(F32)
    low = grad_gain - high
    lane = lax.broadcasted_iota(jnp.int32, (piece_rows, 128), 1)
    gathered[band, :, pl.ds(0, fan_size)] = grad_raw.astype(BF16)
    gathered[band, :, pl.ds(fan_size, 128)] = jnp.where(lane == 0, high, low).astype(BF16)
    ag = []
    for n, (quarter, to) in enumerate(((band, cross), (band, pair), (cross, pair))):
        if n == 2:
            lax.fori_loop(half_groups, group_count - 1, back_step, 0)
            ag[0].wait_recv()
        block = gathered.at[quarter]
        ag.append(copy(block, block, ag_s.at[n], ag_r.at[n], {"space": to}))
        ag[-1].start()
    lax.fori_loop(group_count - 1, group_count, back_step, 0)
    write(grad_ref.at[:, pl.ds(half_cols, half_cols)], grad_hbm.at[:, pl.ds(half_cols, half_cols)])
    ag[1].wait_recv()
    ag[2].wait_recv()
    lane_id = lax.broadcasted_iota(jnp.int32, (piece_rows, owner_rows), 1)
    line_id = lax.broadcasted_iota(jnp.int32, (piece_rows, owner_rows), 0)
    gain_line = jnp.zeros((1, owner_rows), F32)
    for q in range(4):
        write(gathered.at[q, :, pl.ds(0, fan_size)], ws_hbm.at[pl.ds(q * piece_rows, piece_rows), :])
        both = gathered[q, :, pl.ds(fan_size, 128)].astype(F32)
        column = both[:, 0:1] + both[:, 1:2]
        gain_line = gain_line + jnp.sum(
            jnp.where(lane_id == line_id + q * piece_rows, column, 0.0), axis=0, keepdims=True
        )
    gains_ref[...] = gain_line

    @pl.when(band > 0)
    def _():
        up.wait_send()

    @pl.when(band < 3)
    def _():
        down.wait_send()

    for one in outs:
        one.wait()
    for one in wz + list(rc.values()) + rx + wx + rz + wc + ag:
        one.wait_send()


def widen_kernel(
    grad_ref, rounded_ref, gains_ref, grad_out, raw_out, gains_out, held, narrow, wide, line, sems
):
    halves = []
    middle = grad_ref.shape[0] // 2
    for k in range(2):
        at = pl.ds(k * middle, middle)
        halves.append((
            pltpu.make_async_copy(grad_ref.at[at, :], held.at[at, :], sems.at[k]),
            pltpu.make_async_copy(held.at[at, :], grad_out.at[at, :], sems.at[2 + k]),
        ))
    rows = narrow.shape[0] // 2
    for k in range(2):
        at = pl.ds(k * rows, rows)
        halves.append((
            pltpu.make_async_copy(rounded_ref.at[at, :], narrow.at[at, :], sems.at[4 + k]),
            pltpu.make_async_copy(wide.at[at, :], raw_out.at[at, :], sems.at[6 + k]),
        ))
    halves.append((
        pltpu.make_async_copy(gains_ref, line, sems.at[8]),
        pltpu.make_async_copy(line, gains_out, sems.at[9]),
    ))
    order = (2, 3, 0, 1, 4)
    for n in order:
        halves[n][0].start()
    for n in order:
        halves[n][0].wait()
        if n in (2, 3):
            at = pl.ds((n - 2) * rows, rows)
            wide[at, :] = narrow[at, :].astype(F32)
        halves[n][1].start()
    for n in order:
        halves[n][1].wait()


def local_kernel(inputs, cotangent, kernel_raw, kernel_gain):
    images, band_rows, band_cols, chan_count = inputs.shape
    owner_rows, fan_size = kernel_raw.shape
    data_count = lax.axis_size("dp")
    pixels = band_rows * band_cols
    piece_rows = owner_rows // 4
    width = fan_size // 9
    dma = pltpu.SemaphoreType.DMA
    peers = data_count - 1
    vmem = pl.BlockSpec(memory_space=pltpu.VMEM)
    hbm = pl.BlockSpec(memory_space=pltpu.HBM)
    grad, rounded, gains = pl.pallas_call(
        functools.partial(block_kernel, images * data_count, data_count),
        out_shape=(
            jax.ShapeDtypeStruct((pixels, chan_count), BF16),
            jax.ShapeDtypeStruct((owner_rows, fan_size), BF16),
            jax.ShapeDtypeStruct((1, owner_rows), F32),
        ),
        in_specs=[hbm] * 4,
        out_specs=(hbm, hbm, vmem),
        scratch_shapes=[
            pltpu.VMEM((pixels, chan_count), BF16),
            pltpu.VMEM((pixels, chan_count), BF16),
            pltpu.VMEM((owner_rows, fan_size), F32),
            pltpu.VMEM((1, owner_rows), F32),
            pltpu.VMEM((owner_rows, 1), F32),
            pltpu.VMEM((pixels, chan_count), BF16),
            dma((4,)), dma((6,)),
            pltpu.VMEM((2, band_cols, chan_count), BF16),
            pltpu.VMEM((pixels + 2 * band_cols, chan_count), BF16),
            pltpu.VMEM((pixels, 3 * chan_count), BF16),
            pltpu.VMEM((pixels, chan_count), F32),
            pltpu.VMEM((chan_count, fan_size), BF16),
            pltpu.VMEM((chan_count, fan_size), F32),
            pltpu.VMEM((chan_count, fan_size), BF16),
            pltpu.VMEM((2 * data_count, piece_rows, fan_size), BF16),
            pltpu.VMEM((data_count, piece_rows, fan_size), BF16),
            pltpu.VMEM((data_count, piece_rows, fan_size), BF16),
            pltpu.VMEM((4, piece_rows, fan_size + 128), BF16),
            dma((2,)), dma((2,)),
            dma((peers,)), dma((data_count,)),
            dma((peers,)), dma((peers,)),
            dma((2 * peers,)), dma((2 * peers,)),
            dma((2 * data_count,)), dma((2 * data_count,)),
            dma((data_count,)), dma((data_count,)),
            dma((peers,)), dma((data_count,)),
            dma((3,)), dma((3,)),
        ],
        compiler_params=pltpu.CompilerParams(
            collective_id=0, has_side_effects=True, vmem_limit_bytes=60 * 1024 * 1024
        ),
        cost_estimate=pl.CostEstimate(
            flops=4 * pixels * chan_count * fan_size,
            bytes_accessed=8 * pixels * chan_count,
            transcendentals=2 * pixels * chan_count,
        ),
    )(
        inputs.reshape(pixels, chan_count),
        cotangent.reshape(pixels, chan_count),
        kernel_raw,
        kernel_gain.reshape(1, owner_rows),
    )
    grad, grad_raw, grad_gain = pl.pallas_call(
        widen_kernel,
        out_shape=(
            jax.ShapeDtypeStruct((pixels, chan_count), BF16),
            jax.ShapeDtypeStruct((owner_rows, fan_size), F32),
            jax.ShapeDtypeStruct((1, owner_rows), F32),
        ),
        in_specs=[hbm] * 3,
        out_specs=(hbm, hbm, hbm),
        scratch_shapes=[
            pltpu.VMEM((pixels, chan_count), BF16),
            pltpu.VMEM((owner_rows, fan_size), BF16),
            pltpu.VMEM((owner_rows, fan_size), F32),
            pltpu.VMEM((1, owner_rows), F32),
            dma((10,)),
        ],
        compiler_params=pltpu.CompilerParams(vmem_limit_bytes=60 * 1024 * 1024),
    )(grad, rounded, gains)
    return (grad.reshape(inputs.shape), grad_raw, grad_gain.reshape(owner_rows))


def solution(mesh):
    placed = (
        P(("groups", "dp"), "space", None, None),
        P(("groups", "dp"), "space", None, None),
        P("dp", None),
        P("dp"),
    )

    def run(inputs, cotangent, kernel_raw, kernel_gain):
        images, rows, cols, chan_count = inputs.shape
        fan_size = kernel_raw.shape[1]
        data_count = mesh.shape["dp"]
        replicas = mesh.shape["groups"] * data_count
        fits = (
            mesh.shape["space"] == 4
            and data_count == 4
            and mesh.shape["groups"] == 2
            and images == replicas
            and chan_count % (64 * data_count) == 0
            and (chan_count // (fan_size // 9)) % 2 == 0
            and fan_size % (9 * 128) == 0
            and cols % 16 == 0
            and rows % 4 == 0
        )
        return jax.shard_map(
            local_kernel if fits else local,
            mesh=mesh,
            in_specs=placed,
            out_specs=(
                P(("groups", "dp"), "space", None, None),
                P(("groups", "dp"), None),
                P(("groups", "dp")),
            ),
            check_vma=False,
        )(inputs, cotangent, kernel_raw, kernel_gain)

    return run
```
